128 devices in a mesh: row: 16 (over y, x_lo, core), list: 8 (over z, x_hi).
Axes of the slice: x: 4 (x_hi: 2, x_lo: 2; x = x_hi * 2 + x_lo), y: 4, z: 4, core: 2. Of those that a mesh axis runs over, the one named last changes fastest.
Arguments:
- key_rows: bfloat16 [16384, 256], P('row'), may hold values from -88 to 88
- centroids: bfloat16 [49152, 256], P('list'), may hold values from -32 to 32
Outputs:
- new_centroids: bfloat16 [49152, 256], P('list')
- row_potential: float32 [16384], P('row')
- list_potential: float32 [49152], P('list')
The draws below stay inside these ranges and needn't reach their ends.
All inputs are finite; a program needn't handle non-finite values.
Results may differ from the reference program's by a relative error of at most 0.0047.
Values may be sent and summed in bfloat16 or wider, within the bound.
A program may use at most 64 MiB of HBM per device.

```python
import math
import jax
import jax.numpy as jnp
from jax import lax

D = 256
LISTS = 49152
ROWS_DEV = 1024
ITERS = 2
N_ROW = 16


def centroid_parts(key):
    noise = jnp.clip(jax.random.normal(jax.random.fold_in(key, 101), (LISTS, D), jnp.float32), -4.5, 4.5)
    ramp = 3.0 ** (jnp.arange(LISTS, dtype=jnp.float32) / LISTS)
    scale = jnp.exp(jax.random.uniform(jax.random.fold_in(key, 102), (LISTS,), jnp.float32, math.log(0.5), math.log(2.0))) * ramp
    pairs = noise.reshape(LISTS // 2, 2, D)
    leading = pairs[:, 0]
    trailing = pairs[:, 1]
    noise = jnp.stack([leading, trailing], axis=1).reshape(LISTS, D)
    scale_pairs = scale.reshape(LISTS // 2, 2)
    scale_trail = scale_pairs[:, 1]
    scale = jnp.stack([scale_pairs[:, 0], scale_trail], axis=1).reshape(LISTS)
    return (noise, scale)


def draw_centroids(key, part):
    noise, scale = centroid_parts(key)
    return (noise * scale[:, None]).astype(jnp.bfloat16)


def draw_key_rows(key, part):
    n_keys = ROWS_DEV * N_ROW
    ramp = 3.0 ** (jnp.arange(n_keys, dtype=jnp.float32) / n_keys)
    key = jax.random.fold_in(key, 5)
    row_scale = jnp.exp(jax.random.uniform(jax.random.fold_in(key, 11), (n_keys,), jnp.float32, math.log(0.5), math.log(2.0))) * ramp
    values = jnp.clip(jax.random.normal(jax.random.fold_in(key, 1), (n_keys, D), jnp.float32), -4.5, 4.5) * row_scale[:, None]
    return values.astype(jnp.bfloat16)


def setup_inputs(seed: int = 0) -> dict:
    keys = jax.random.split(jax.random.key(seed), 3)
    return {
        "key_rows": draw_key_rows(jax.random.fold_in(keys[2], 71), 0),
        "centroids": draw_centroids(jax.random.fold_in(keys[2], 71), 0),
    }


def scored_tile(key_rows, cent_tile):
    factor = 2.0 / math.sqrt(key_rows.shape[1])
    return lax.dot_general(key_rows, cent_tile, (((1,), (1,)), ((), ())), preferred_element_type=jnp.float32) * factor

def reference(key_rows, centroids):
    n_keys = key_rows.shape[0]
    n_lists = centroids.shape[0]
    span = math.gcd(n_lists, 1024)
    tiles = centroids.reshape(n_lists // span, span, centroids.shape[1])
    list_potential = jnp.zeros((n_lists,), jnp.float32)
    row_potential = jnp.zeros((n_keys,), jnp.float32)
    for sweep in range(ITERS):
        pots = list_potential.reshape(n_lists // span, span)

        def advance(carry, item):
            peak, total = carry
            scored = scored_tile(key_rows, item[0]) + item[1][None, :]
            top = jnp.maximum(peak, lax.optimization_barrier(jnp.max(scored, axis=1)))
            total = total * jnp.exp(peak - top) + lax.optimization_barrier(jnp.sum(jnp.exp(scored - top[:, None]), axis=1))
            return ((top, total), None)
        start = (jnp.full((n_keys,), -1e+30, jnp.float32), jnp.zeros((n_keys,), jnp.float32))
        (peak, total), unused = lax.scan(advance, start, (tiles, pots))
        row_potential = -math.log(n_keys) - (peak + jnp.log(total))

        def column_stats(tile):
            scored = scored_tile(key_rows, tile) + row_potential[:, None]
            top = lax.optimization_barrier(jnp.max(scored, axis=0))
            return top + jnp.log(lax.optimization_barrier(jnp.sum(jnp.exp(scored - top[None, :]), axis=0)))
        column_lse = lax.map(column_stats, tiles).reshape(n_lists)
        list_potential = -math.log(n_lists) - column_lse
    pots = list_potential.reshape(n_lists // span, span)

    def update_tile(item):
        scored = scored_tile(key_rows, item[0])
        weights = jnp.exp(scored + row_potential[:, None] + item[1][None, :] + math.log(n_lists)).astype(jnp.bfloat16)
        return lax.dot_general(weights, key_rows, (((0,), (0,)), ((), ())), preferred_element_type=jnp.float32)
    summed = lax.map(update_tile, (tiles, pots)).reshape(n_lists, centroids.shape[1])
    return (summed.astype(jnp.bfloat16), row_potential, list_potential)
```

```python
import math

import jax
import jax.numpy as jnp
from jax import lax
from jax.experimental import pallas as pl
from jax.experimental.pallas import tpu as pltpu
from jax.sharding import PartitionSpec as P

MESH = pl.DeviceIdType.MESH
f32 = jnp.float32
bf16 = jnp.bfloat16
LOG2E = math.log2(math.e)
LN2 = math.log(2.0)

D = 256
SCALE = 2.0 / math.sqrt(D) * LOG2E
NK = 1024
NL = 6144
W = 512
NT = NL // W
N_ROW, N_LIST, CHIPS, CORES = 16, 8, 8, 2
SHARE = NL // CHIPS
BLOCKS = SHARE // 128
LB = 256
NCH = SHARE // LB
KT = 1024
STEPS = CHIPS * NK // (2 * KT)
LOG2_KEYS = math.log2(NK * N_ROW)
LOG2_LISTS = math.log2(NL * N_LIST)
NT_DIMS = (((1,), (1,)), ((), ()))
NN_DIMS = (((1,), (0,)), ((), ()))


def tree(op, xs):
    xs = list(xs)
    while len(xs) > 1:
        ys = [op(a, b) for a, b in zip(xs[::2], xs[1::2])]
        if len(xs) % 2:
            ys.append(xs[-1])
        xs = ys
    return xs[0]


def log2(x):
    return jnp.log(x) * LOG2E


def fold(op, x):
    return tree(op, [x[8 * i : 8 * i + 8] for i in range(x.shape[0] // 8)])


def row_pass(keys, cents, scores, peak, total):
    peak[...] = jnp.full(peak.shape, -1e30, f32)
    total[...] = jnp.zeros(total.shape, f32)
    rb = 32

    def body(i, carry):
        for half in range(2):
            t = 2 * i + half
            lists = pl.ds(pl.multiple_of(t * W, W), W)
            s = lax.dot_general(keys[...], cents[lists, :], NT_DIMS, preferred_element_type=f32) * SCALE
            scores[t] = s
            for b in range(NK // rb):
                rows = slice(b * rb, (b + 1) * rb)
                xs = [s[rows, v * 128 : (v + 1) * 128] for v in range(W // 128)]
                before = peak[rows, :]
                top = jnp.maximum(before, tree(jnp.maximum, xs))
                sums = tree(jnp.add, [jnp.exp2(x - top) for x in xs])
                total[rows, :] = total[rows, :] * jnp.exp2(before - top) + sums
                peak[rows, :] = top
        return carry

    lax.fori_loop(0, NT // 2, body, 0)


def column_pass(scores, row_pot, stats, first, last):
    rb = 256

    def body(i, carry):
        for v in range(W // 128):
            lanes = slice(v * 128, (v + 1) * 128)
            tops = []
            for b in range(NK // rb):
                rows = slice(b * rb, (b + 1) * rb)
                x = scores[i, rows, lanes] + row_pot[rows, :]
                scores[i, rows, lanes] = x
                tops.append(fold(jnp.maximum, x))
            top = jnp.max(tree(jnp.maximum, tops), axis=0, keepdims=True)
            sums = []
            for b in range(NK // rb):
                rows = slice(b * rb, (b + 1) * rb)
                e = jnp.exp2(scores[i, rows, lanes] - top)
                scores[i, rows, lanes] = e
                sums.append(fold(jnp.add, e))
            total = jnp.sum(tree(jnp.add, sums), axis=0, keepdims=True)
            j = i * (W // 128) + v
            q, at = lax.div(j, BLOCKS), lax.rem(j, BLOCKS)
            stats[pl.ds(q, 1), 0, pl.ds(at, 1), :] = top[None]
            stats[pl.ds(q, 1), 1, pl.ds(at, 1), :] = total[None]
        return carry

    lax.fori_loop(first, last, body, 0)


def row_sums(scores, gain, total):
    rb, group = 64, 4

    def body(i, carry):
        def at(b):
            return pl.ds(pl.multiple_of(i * rb + 8 * b, 8), 8)

        def inner(c, accs):
            accs = list(accs)
            for t in range(group):
                for v in range(W // 128):
                    lanes = slice(v * 128, (v + 1) * 128)
                    g = gain[c * group + t, :, lanes]
                    for b in range(rb // 8):
                        accs[b] = accs[b] + scores[c * group + t, at(b), lanes] * g
            return tuple(accs)

        zero = jnp.zeros((8, 128), f32)
        accs = lax.fori_loop(0, NT // group, inner, (zero,) * (rb // 8))
        for b in range(rb // 8):
            total[at(b), :] = accs[b]
        return carry

    lax.fori_loop(0, NK // rb, body, 0)


def column_sums(scores, factor, sums):
    rb = 128

    def body(i, carry):
        accs = [[] for _ in range(W // 128)]
        for b in range(NK // rb):
            rows = slice(b * rb, (b + 1) * rb)
            u = factor[rows, :]
            for v in range(W // 128):
                part = fold(jnp.add, scores[i, rows, v * 128 : (v + 1) * 128] * u)
                accs[v] = part if b == 0 else accs[v] + part
        for v in range(W // 128):
            j = i * (W // 128) + v
            q, at = lax.div(j, BLOCKS), lax.rem(j, BLOCKS)
            sums[pl.ds(q, 1), pl.ds(at, 1), :] = jnp.sum(accs[v], axis=0, keepdims=True)[None]
        return carry

    lax.fori_loop(0, NT, body, 0)


def spread(compact, n, out):
    for b in range(n):
        out[b * 128 : (b + 1) * 128, :] = jnp.broadcast_to(compact[b : b + 1, :], (128, 128)).T


def remote(src, dst, send, recv, target):
    return pltpu.make_async_remote_copy(
        src_ref=src, dst_ref=dst, send_sem=send, recv_sem=recv, device_id=target, device_id_type=MESH
    )


class Gather:
    def __init__(self, at, send, recv, y, x, core, twin=False, own=None):
        self.at, self.send, self.recv, self.twin = at, send, recv, twin
        self.core = core
        self.own = own

        def chip(dy, flip):
            return lax.rem(y + dy + 4, 4) * 2 + (1 - x if flip else x)

        self.chip = chip
        self.up = {"row": chip(1, False) * 2 + core}
        self.down = {"row": chip(-1, False) * 2 + core}
        self.side = {"row": chip(0, True) * 2 + core}
        self.other = {"row": chip(0, False) * 2 + 1 - core}
        self.moves = [
            (self.up, (0, False), (-1, False), None),
            (self.down, (0, False), (1, False), None),
            (self.side, (0, False), (0, True), None),
            (self.up, (-1, False), (-2, False), 0),
            (self.down, (1, False), (2, False), 1),
            (self.up, (0, True), (-1, True), None),
            (self.down, (0, True), (1, True), None),
            (self.side, (-2, False), (2, True), 0),
            (self.side, (2, False), (2, True), 1),
        ]

    def source(self, block, part):
        if self.own is not None and block == (0, False):
            return self.own
        return self.at(self.chip(*block), part)

    def copy(self, m):
        target, sent, _, part = self.moves[m]
        place = self.at(self.chip(*sent), part)
        return remote(self.source(sent, part), place, self.send.at[m], self.recv.at[m], target)

    def arrival(self, m):
        target, _, came, part = self.moves[m]
        place = self.at(self.chip(*came), part)
        return remote(place, place, self.send.at[m], self.recv.at[m], target)

    def hand(self, m):
        block, part = ((0, False), None) if m == 9 else self.moves[m][2:]
        place = self.at(self.chip(*block), part)
        return remote(self.source(block, part), place, self.send.at[10 + m], self.recv.at[10 + m], self.other)

    def handed(self, m):
        block, part = ((0, False), None) if m == 9 else self.moves[m][2:]
        place = self.at(self.chip(*block), part, 1 - self.core)
        return remote(place, place, self.send.at[10 + m], self.recv.at[10 + m], self.other)

    def take(self, arrivals, sends):
        for m in arrivals:
            self.arrival(m).wait_recv()
            for s in sends.get(m, ()):
                self.copy(s).start()
            if self.twin:
                self.hand(m).start()

    def stage1(self):
        for m in (0, 1, 2):
            self.copy(m).start()
        if self.twin:
            self.hand(9).start()

    def stage2(self):
        self.take((0, 1, 2), {0: (3,), 1: (4,), 2: (5, 6)})

    def stage3(self):
        self.take((3, 4), {3: (7,), 4: (8,)})

    def stage4(self):
        self.take((5, 6, 7, 8), {})

    def finish(self):
        for m in range(9):
            self.copy(m).wait_send()
        if self.twin:
            for m in range(10):
                self.hand(m).wait_send()
                self.handed(m).wait_recv()


def kernel(
    keys, cents, new_ref, rowpot_ref, listpot_ref,
    scores, peak, total, row_pot, gain, stats, sums, pots, pots2, from_list1, from_list3, from_row2, from_row4,
    row_all, keys_all, row_lanes, list_lanes, sa, sb, acc, came, done,
    list1_s, list1_r, list3_s, list3_r, row2_s, row2_r, row4_s, row4_r, pot_s, pot_r, pot2_s, pot2_r, all_s, all_r,
    keys_s, keys_r, twin_s, twin_r, out_s, out_r, here,
):
    row, lst = lax.axis_index("row"), lax.axis_index("list")
    core, chip = lax.rem(row, 2), lax.div(row, 2)
    x, y = lax.rem(chip, 2), lax.div(chip, 2)

    barrier = pltpu.get_barrier_semaphore()
    for k in range(1, N_ROW):
        pl.semaphore_signal(barrier, inc=1, device_id={"row": lax.rem(row + k, N_ROW)}, device_id_type=MESH)
    for k in range(1, N_LIST):
        pl.semaphore_signal(barrier, inc=1, device_id={"list": lax.rem(lst + k, N_LIST)}, device_id_type=MESH)
    stats[...] = jnp.zeros(stats.shape, f32)
    sums[...] = jnp.zeros(sums.shape, f32)
    keys_all[chip] = keys[...]
    pl.semaphore_wait(barrier, N_ROW + N_LIST - 2)

    def keys_at(q, part):
        return keys_all.at[q] if part is None else keys_all.at[q, pl.ds(part * (NK // 2), NK // 2)]

    gather = Gather(keys_at, keys_s, keys_r, y, x, core)
    gather.stage1()

    def to_list(buf, send, recv):
        for k in range(1, N_LIST):
            remote(buf.at[lst], buf.at[lst], send.at[k], recv.at[lst], {"list": lax.rem(lst + k, N_LIST)}).start()

    def from_list(buf, send, recv):
        for k in range(1, N_LIST):
            src = lax.rem(lst + k, N_LIST)
            remote(buf.at[src], buf.at[src], send.at[k], recv.at[src], {"list": src}).wait_recv()
        for k in range(1, N_LIST):
            remote(buf.at[lst], buf.at[lst], send.at[k], recv.at[lst], {"list": lax.rem(lst + k, N_LIST)}).wait_send()

    def to_row(src_of, buf, send, recv):
        for k in range(1, N_ROW):
            to = lax.rem(row + k, N_ROW)
            remote(src_of.at[lax.div(to, 2)], buf.at[row], send.at[k], recv.at[row], {"row": to}).start()

    def from_row(src_of, buf, send, recv):
        for k in range(1, N_ROW):
            src = lax.rem(row + k, N_ROW)
            remote(buf.at[src], buf.at[src], send.at[k], recv.at[src], {"row": src}).wait_recv()
        for k in range(1, N_ROW):
            to = lax.rem(row + k, N_ROW)
            remote(src_of.at[lax.div(to, 2)], buf.at[row], send.at[k], recv.at[row], {"row": to}).wait_send()

    def to_chips(buf, send, recv):
        for k in range(1, CHIPS):
            to = lax.rem(chip + k, CHIPS) * 2 + core
            remote(buf.at[chip], buf.at[chip], send.at[k], recv.at[chip], {"row": to}).start()

    def from_chips(buf, send, recv):
        for k in range(1, CHIPS):
            src = lax.rem(chip + k, CHIPS)
            remote(buf.at[src], buf.at[src], send.at[k], recv.at[src], {"row": src * 2 + core}).wait_recv()
        for k in range(1, CHIPS):
            to = lax.rem(chip + k, CHIPS) * 2 + core
            remote(buf.at[chip], buf.at[chip], send.at[k], recv.at[chip], {"row": to}).wait_send()

    row_pass(keys, cents, scores, peak, total)
    for b in range(NK // 128):
        rows = slice(b * 128, (b + 1) * 128)
        top = peak[rows, :].T
        best = jnp.max(top, axis=0, keepdims=True)
        part = jnp.sum(total[rows, :].T * jnp.exp2(top - best), axis=0, keepdims=True)
        from_list1[lst, 0, b : b + 1, :] = best
        from_list1[lst, 1, b : b + 1, :] = part
    to_list(from_list1, list1_s, list1_r)
    from_list(from_list1, list1_s, list1_r)
    best = tree(jnp.maximum, [from_list1[k, 0] for k in range(N_LIST)])
    whole = tree(jnp.add, [from_list1[k, 1] * jnp.exp2(from_list1[k, 0] - best) for k in range(N_LIST)])
    row1 = -LOG2_KEYS - (best + log2(whole))
    spread(row1, NK // 128, row_pot)

    column_pass(scores, row_pot, stats, 0, 4)
    gather.stage2()
    column_pass(scores, row_pot, stats, 4, NT)
    from_row2[row] = stats[chip]
    to_row(stats, from_row2, row2_s, row2_r)
    from_row(stats, from_row2, row2_s, row2_r)
    best = tree(jnp.maximum, [from_row2[k, 0] for k in range(N_ROW)])
    whole = tree(jnp.add, [from_row2[k, 1] * jnp.exp2(from_row2[k, 0] - best) for k in range(N_ROW)])
    pots[chip] = -LOG2_LISTS - (best + log2(whole))
    to_chips(pots, pot_s, pot_r)
    gather.stage3()
    from_chips(pots, pot_s, pot_r)

    for q in range(CHIPS):
        g = jnp.exp2(stats[q, 0] + pots[q])
        stats[q, 1] = g
        for b in range(BLOCKS):
            j = q * BLOCKS + b
            v = j % (W // 128)
            gain[j // (W // 128), :, v * 128 : (v + 1) * 128] = jnp.broadcast_to(g[b : b + 1, :], (8, 128))
    row_sums(scores, gain, total)
    for b in range(NK // 128):
        from_list3[lst, b : b + 1, :] = jnp.sum(total[b * 128 : (b + 1) * 128, :].T, axis=0, keepdims=True)
    to_list(from_list3, list3_s, list3_r)
    from_list(from_list3, list3_s, list3_r)
    delta = -LOG2_KEYS - log2(tree(jnp.add, [from_list3[k] for k in range(N_LIST)]))
    row2 = row1 + delta
    row_all[chip] = row2
    to_chips(row_all, all_s, all_r)
    rowpot_ref[...] = row2 * LN2
    spread(jnp.exp2(delta), NK // 128, row_pot)

    column_sums(scores, row_pot, sums)
    for q in range(CHIPS):
        sums[q] = sums[q] * stats[q, 1]
    from_row4[row] = sums[chip]
    to_row(sums, from_row4, row4_s, row4_r)
    gather.stage4()
    from_chips(row_all, all_s, all_r)
    for q in range(CHIPS):
        for b in range(NK // 128):
            row_lanes[:, (q * 8 + b) * 128 : (q * 8 + b + 1) * 128] = row_all[q, b : b + 1, :]
    from_row(sums, from_row4, row4_s, row4_r)
    list2 = pots[chip] - LOG2_LISTS - log2(tree(jnp.add, [from_row4[k] for k in range(N_ROW)]))
    pots2[chip] = list2
    to_chips(pots2, pot2_s, pot2_r)
    spread(list2 + LOG2_LISTS, BLOCKS, list_lanes)
    gather.finish()

    def chunk_at(ch):
        def at(q, part, of=core):
            base = q * SHARE + ch * LB + of * (LB // 2)
            if part is None:
                return new_ref.at[pl.ds(pl.multiple_of(base, LB // 2), LB // 2)]
            return new_ref.at[pl.ds(pl.multiple_of(base + part * (LB // 4), LB // 4), LB // 4)]

        return at

    outs = [
        Gather(chunk_at(ch), out_s.at[ch], out_r.at[ch], y, x, core, twin=True, own=done.at[ch]) for ch in range(NCH)
    ]
    twin = {"row": chip * 2 + 1 - core}
    mine = pl.multiple_of(core * (LB // 2), LB // 2)
    theirs = pl.multiple_of((1 - core) * (LB // 2), LB // 2)

    def swap(ch):
        return remote(acc.at[ch, pl.ds(theirs, LB // 2)], came.at[ch], twin_s.at[ch], twin_r.at[ch], twin)

    def keep(ch):
        return pltpu.make_async_copy(done.at[ch], chunk_at(ch)(chip, None), here.at[ch])

    def begin(ch):
        swap(ch).wait()
        done[ch] = (acc[ch, pl.ds(mine, LB // 2), :] + came[ch]).astype(bf16)
        outs[ch].stage1()
        keep(ch).start()

    def tile(t):
        return keys_all[lax.div(t * KT, NK)]

    def mm1(ch, t):
        c = cents[pl.ds(pl.multiple_of(chip * SHARE + ch * LB, LB), LB), :]
        return lax.dot_general(c, tile(t), NT_DIMS, preferred_element_type=f32)

    def weigh(s_ref, ch, t):
        c = list_lanes[pl.ds(pl.multiple_of(ch * LB, LB), LB), :]
        out = []
        for v in range(KT // 128):
            r = row_lanes[:, pl.ds(pl.multiple_of(t * KT + v * 128, 128), 128)]
            s = s_ref[:, v * 128 : (v + 1) * 128] * SCALE
            out.append(jnp.exp2((s + r) + c).astype(bf16))
        return jnp.concatenate(out, axis=1)

    def mm2(w, t):
        return lax.dot_general(w, tile(t), NN_DIMS, preferred_element_type=f32)

    acc[...] = jnp.zeros(acc.shape, f32)
    sa[...] = mm1(0, 0)

    def step(i, carry):
        ch, t = lax.div(i, STEPS), 2 * lax.rem(i, STEPS)
        nxt = lax.rem(i + 1, NCH * STEPS)
        sb[...] = mm1(ch, t + 1)
        first = mm2(weigh(sa, ch, t), t)
        sa[...] = mm1(lax.div(nxt, STEPS), 2 * lax.rem(nxt, STEPS))
        acc[ch] += first + mm2(weigh(sb, ch, t + 1), t + 1)

        def when(n, *jobs):
            @pl.when(i == n)
            def _():
                for job in jobs:
                    job()

        when(3, lambda: swap(0).start())
        when(4, lambda: begin(0))
        when(6, lambda: outs[0].stage2())
        when(7, lambda: swap(1).start())
        when(8, lambda: begin(1), lambda: outs[0].stage3())
        when(10, lambda: outs[1].stage2(), lambda: outs[0].stage4())
        return carry

    lax.fori_loop(0, NCH * STEPS, step, 0)
    swap(2).start()
    outs[1].stage3()
    from_chips(pots2, pot2_s, pot2_r)
    for q in range(CHIPS):
        listpot_ref[q * BLOCKS : (q + 1) * BLOCKS, :] = pots2[q, 0:BLOCKS, :] * LN2
    begin(2)
    outs[1].stage4()
    outs[2].stage2()
    outs[2].stage3()
    outs[2].stage4()
    for ch in range(NCH):
        keep(ch).wait()
        outs[ch].finish()


def local(key_rows, centroids):
    vmem = pl.BlockSpec(memory_space=pltpu.VMEM)
    dma = pltpu.SemaphoreType.DMA
    small = (8, 128)
    new, row_pot, list_pot = pl.pallas_call(
        kernel,
        out_shape=(
            jax.ShapeDtypeStruct((NL, D), bf16),
            jax.ShapeDtypeStruct(small, f32),
            jax.ShapeDtypeStruct((NL // 128, 128), f32),
        ),
        in_specs=[vmem, vmem],
        out_specs=(pl.BlockSpec(memory_space=pl.ANY), vmem, vmem),
        scratch_shapes=[
            pltpu.VMEM((NT, NK, W), f32),
            pltpu.VMEM((NK, 128), f32),
            pltpu.VMEM((NK, 128), f32),
            pltpu.VMEM((NK, 128), f32),
            pltpu.VMEM((NT, 8, W), f32),
            pltpu.VMEM((CHIPS, 2, *small), f32),
            pltpu.VMEM((CHIPS, *small), f32),
            pltpu.VMEM((CHIPS, *small), f32),
            pltpu.VMEM((CHIPS, *small), f32),
            pltpu.VMEM((N_LIST, 2, *small), f32),
            pltpu.VMEM((N_LIST, *small), f32),
            pltpu.VMEM((N_ROW, 2, *small), f32),
            pltpu.VMEM((N_ROW, *small), f32),
            pltpu.VMEM((CHIPS, *small), f32),
            pltpu.VMEM((CHIPS, NK, D), bf16),
            pltpu.VMEM((1, CHIPS * NK), f32),
            pltpu.VMEM((SHARE, 128), f32),
            pltpu.VMEM((LB, KT), f32),
            pltpu.VMEM((LB, KT), f32),
            pltpu.VMEM((NCH, LB, D), f32),
            pltpu.VMEM((NCH, LB // 2, D), f32),
            pltpu.VMEM((NCH, LB // 2, D), bf16),
            dma((N_LIST,)), dma((N_LIST,)), dma((N_LIST,)), dma((N_LIST,)),
            dma((N_ROW,)), dma((N_ROW,)), dma((N_ROW,)), dma((N_ROW,)),
            dma((CHIPS,)), dma((CHIPS,)), dma((CHIPS,)), dma((CHIPS,)), dma((CHIPS,)), dma((CHIPS,)),
            dma((9,)), dma((9,)), dma((NCH,)), dma((NCH,)), dma((NCH, 20)), dma((NCH, 20)), dma((NCH,)),
        ],
        compiler_params=pltpu.CompilerParams(
            collective_id=0, has_side_effects=True, vmem_limit_bytes=60 * 2**20
        ),
        name="sinkhorn",
    )(key_rows, centroids)
    return new, row_pot.reshape(NK), list_pot.reshape(NL)


def solution(mesh):
    return jax.shard_map(
        local,
        mesh=mesh,
        in_specs=(P("row", None), P("list", None)),
        out_specs=(P("list", None), P("row"), P("list")),
        check_vma=False,
    )
```

```python
import math

import jax
import jax.numpy as jnp
from jax import lax
from jax.experimental import pallas as pl
from jax.experimental.pallas import tpu as pltpu
from jax.sharding import PartitionSpec as P

MESH = pl.DeviceIdType.MESH
f32 = jnp.float32
bf16 = jnp.bfloat16
LOG2E = math.log2(math.e)
LN2 = math.log(2.0)

D = 256
SCALE = 2.0 / math.sqrt(D) * LOG2E
NK = 1024
NL = 6144
W = 512
NT = NL // W
N_ROW, N_LIST, SEATS = 16, 8, 8
SHARE = NL // SEATS
BLOCKS = SHARE // 128
LB = 256
NCH = SHARE // LB
KT = 1024
STEPS = SEATS * NK // (2 * KT)
LOG2_KEYS = math.log2(NK * N_ROW)
LOG2_LISTS = math.log2(NL * N_LIST)
NT_DIMS = (((1,), (1,)), ((), ()))
NN_DIMS = (((1,), (0,)), ((), ()))


def tree(op, xs):
    xs = list(xs)
    while len(xs) > 1:
        ys = [op(a, b) for a, b in zip(xs[::2], xs[1::2])]
        if len(xs) % 2:
            ys.append(xs[-1])
        xs = ys
    return xs[0]


def log2(x):
    return jnp.log(x) * LOG2E


def fold(op, x):
    return tree(op, [x[8 * i : 8 * i + 8] for i in range(x.shape[0] // 8)])


def row_pass(keys, cents, scores, peak, total, first, last):
    rb = 32

    def body(i, carry):
        for half in range(2):
            t = 2 * i + half
            lists = pl.ds(pl.multiple_of(t * W, W), W)
            s = lax.dot_general(keys[...], cents[lists, :], NT_DIMS, preferred_element_type=f32) * SCALE
            scores[t] = s
            for b in range(NK // rb):
                rows = slice(b * rb, (b + 1) * rb)
                xs = [s[rows, v * 128 : (v + 1) * 128] for v in range(W // 128)]
                before = peak[rows, :]
                top = jnp.maximum(before, tree(jnp.maximum, xs))
                sums = tree(jnp.add, [jnp.exp2(x - top) for x in xs])
                total[rows, :] = total[rows, :] * jnp.exp2(before - top) + sums
                peak[rows, :] = top
        return carry

    lax.fori_loop(first // 2, last // 2, body, 0)


def column_pass(scores, row_pot, stats, first, last):
    rb = 256

    def body(i, carry):
        for v in range(W // 128):
            lanes = slice(v * 128, (v + 1) * 128)
            tops = []
            for b in range(NK // rb):
                rows = slice(b * rb, (b + 1) * rb)
                x = scores[i, rows, lanes] + row_pot[rows, :]
                scores[i, rows, lanes] = x
                tops.append(fold(jnp.maximum, x))
            top = jnp.max(tree(jnp.maximum, tops), axis=0, keepdims=True)
            sums = []
            for b in range(NK // rb):
                rows = slice(b * rb, (b + 1) * rb)
                e = jnp.exp2(scores[i, rows, lanes] - top)
                scores[i, rows, lanes] = e
                sums.append(fold(jnp.add, e))
            total = jnp.sum(tree(jnp.add, sums), axis=0, keepdims=True)
            j = i * (W // 128) + v
            q, at = lax.div(j, BLOCKS), lax.rem(j, BLOCKS)
            stats[pl.ds(q, 1), 0, pl.ds(at, 1), :] = top[None]
            stats[pl.ds(q, 1), 1, pl.ds(at, 1), :] = total[None]
        return carry

    lax.fori_loop(first, last, body, 0)


def row_sums(scores, gain, total):
    rb, group = 64, 4

    def body(i, carry):
        def at(b):
            return pl.ds(pl.multiple_of(i * rb + 8 * b, 8), 8)

        def inner(c, accs):
            accs = list(accs)
            for t in range(group):
                for v in range(W // 128):
                    lanes = slice(v * 128, (v + 1) * 128)
                    g = gain[c * group + t, :, lanes]
                    for b in range(rb // 8):
                        accs[b] = accs[b] + scores[c * group + t, at(b), lanes] * g
            return tuple(accs)

        zero = jnp.zeros((8, 128), f32)
        accs = lax.fori_loop(0, NT // group, inner, (zero,) * (rb // 8))
        for b in range(rb // 8):
            total[at(b), :] = accs[b]
        return carry

    lax.fori_loop(0, NK // rb, body, 0)


def column_sums(scores, factor, sums):
    rb = 128

    def body(i, carry):
        accs = [[] for _ in range(W // 128)]
        for b in range(NK // rb):
            rows = slice(b * rb, (b + 1) * rb)
            u = factor[rows, :]
            for v in range(W // 128):
                part = fold(jnp.add, scores[i, rows, v * 128 : (v + 1) * 128] * u)
                accs[v] = part if b == 0 else accs[v] + part
        for v in range(W // 128):
            j = i * (W // 128) + v
            q, at = lax.div(j, BLOCKS), lax.rem(j, BLOCKS)
            sums[pl.ds(q, 1), pl.ds(at, 1), :] = jnp.sum(accs[v], axis=0, keepdims=True)[None]
        return carry

    lax.fori_loop(0, NT, body, 0)


def spread(compact, n, out):
    for b in range(n):
        out[b * 128 : (b + 1) * 128, :] = jnp.broadcast_to(compact[b : b + 1, :], (128, 128)).T


def remote(src, dst, send, recv, target):
    return pltpu.make_async_remote_copy(
        src_ref=src, dst_ref=dst, send_sem=send, recv_sem=recv, device_id=target, device_id_type=MESH
    )


class Gather:
    def __init__(self, at, send, recv, y, x, core, own, ring=False):
        self.at, self.send, self.recv = at, send, recv
        self.y, self.x, self.core, self.own, self.ring = y, x, core, own, ring

        def device(dy, flip, of=core):
            return {"row": (lax.rem(y + dy + 4, 4) * 2 + (1 - x if flip else x)) * 2 + of}

        up, down, side = device(1, False), device(-1, False), device(0, True)
        self.other = device(0, False, 1 - core)
        self.moves = [
            (up, (0, False), (-1, False), None),
            (down, (0, False), (1, False), None),
            (up, (-1, False), (-2, False), 0),
            (down, (1, False), (2, False), 1),
            (side, (0, False), (0, True), None),
            (up, (0, True), (-1, True), None),
            (down, (0, True), (1, True), None),
            (side, (-2, False), (2, True), 0),
            (side, (2, False), (2, True), 1),
        ]
        self.used = range(4) if ring else range(9)

    def place(self, block, part, *of):
        dy, flip = block
        return self.at(lax.rem(self.y + dy + 4, 4), 1 - self.x if flip else self.x, part, *of)

    def source(self, block, part):
        return self.own if block == (0, False) else self.place(block, part)

    def copy(self, m):
        target, sent, _, part = self.moves[m]
        return remote(self.source(sent, part), self.place(sent, part), self.send.at[m], self.recv.at[m], target)

    def arrival(self, m):
        target, _, came, part = self.moves[m]
        place = self.place(came, part)
        return remote(place, place, self.send.at[m], self.recv.at[m], target)

    def brought(self, m):
        return ((0, False), None) if m == 9 else self.moves[m][2:]

    def hand(self, m):
        block, part = self.brought(m)
        return remote(
            self.source(block, part), self.place(block, part), self.send.at[10 + m], self.recv.at[10 + m], self.other
        )

    def handed(self, m):
        block, part = self.brought(m)
        place = self.place(block, part, 1 - self.core)
        return remote(place, place, self.send.at[10 + m], self.recv.at[10 + m], self.other)

    def take(self, m, *sends):
        if m in self.used:
            self.arrival(m).wait_recv()
            for n in sends:
                if n in self.used:
                    self.copy(n).start()
            self.hand(m).start()

    def stage1(self):
        for m in (0, 1, 4):
            if m in self.used:
                self.copy(m).start()
        self.hand(9).start()

    def stage2(self):
        self.take(0, 2)
        self.take(1, 3)
        self.take(4, 5, 6)

    def stage3(self):
        self.take(2, 7)
        self.take(3, 8)

    def stage4(self):
        for m in (5, 6, 7, 8):
            self.take(m)

    def arrive(self):
        for m in (*self.used, 9):
            self.handed(m).wait_recv()

    def sent(self):
        for m in self.used:
            self.copy(m).wait_send()
        for m in (*self.used, 9):
            self.hand(m).wait_send()


def kernel(
    keys, cents, new_ref, rowpot_ref, listpot_ref,
    scores, peak, total, row_pot, gain, gains, stats, sums, pots, pots2, from_list1, from_list3, from_row2, from_row4,
    row_all, keys_all, row_lanes, list_lanes, sa, sb, acc, give, came, done,
    list1_s, list1_r, list3_s, list3_r, row2_s, row2_r, row4_s, row4_r, pot_s, pot_r, pot2_s, pot2_r, all_s, all_r,
    keys_s, keys_r, twin_s, twin_r, out_s, out_r, here,
):
    row, lst = lax.axis_index("row"), lax.axis_index("list")
    core, x, y = lax.rem(row, 2), lax.rem(lax.div(row, 2), 2), lax.div(row, 4)
    seat = y * 2 + core

    def device(at, x):
        return (lax.div(at, 2) * 2 + x) * 2 + lax.rem(at, 2)

    def seat_of(device):
        return lax.div(device, 4) * 2 + lax.rem(device, 2)

    barrier = pltpu.get_barrier_semaphore()
    for k in range(1, N_ROW):
        pl.semaphore_signal(barrier, inc=1, device_id={"row": lax.rem(row + k, N_ROW)}, device_id_type=MESH)
    for k in range(1, N_LIST):
        pl.semaphore_signal(barrier, inc=1, device_id={"list": lax.rem(lst + k, N_LIST)}, device_id_type=MESH)
    stats[...] = jnp.zeros(stats.shape, f32)
    sums[...] = jnp.zeros(sums.shape, f32)
    peak[...] = jnp.full(peak.shape, -1e30, f32)
    total[...] = jnp.zeros(total.shape, f32)
    keys_all[seat] = keys[...]
    row_pass(keys, cents, scores, peak, total, 0, 4)
    pl.semaphore_wait(barrier, N_ROW + N_LIST - 2)

    def keys_at(y, x, part, of=core):
        at = y * 2 + of
        return keys_all.at[at] if part is None else keys_all.at[at, pl.ds(part * (NK // 2), NK // 2)]

    gather = Gather(keys_at, keys_s, keys_r, y, x, core, keys, ring=True)
    gather.stage1()
    sent = []

    def start(copies):
        for copy in copies:
            copy.start()
            sent.append(copy)

    def to_list(buf, send, recv):
        start(
            remote(buf.at[lst], buf.at[lst], send.at[k], recv.at[lst], {"list": lax.rem(lst + k, N_LIST)})
            for k in range(1, N_LIST)
        )

    def from_list(buf, send, recv):
        for k in range(1, N_LIST):
            src = lax.rem(lst + k, N_LIST)
            remote(buf.at[src], buf.at[src], send.at[k], recv.at[src], {"list": src}).wait_recv()

    def to_row(src_of, buf, send, recv):
        to = [lax.rem(row + k, N_ROW) for k in range(1, N_ROW)]
        start(
            remote(src_of.at[seat_of(t)], buf.at[row], send.at[k + 1], recv.at[row], {"row": t})
            for k, t in enumerate(to)
        )

    def from_row(buf, send, recv):
        for k in range(1, N_ROW):
            src = lax.rem(row + k, N_ROW)
            remote(buf.at[src], buf.at[src], send.at[k], recv.at[src], {"row": src}).wait_recv()

    def to_seats(buf, send, recv):
        to = [lax.rem(seat + k, SEATS) for k in range(1, SEATS)]
        start(
            remote(buf.at[seat], buf.at[seat], send.at[k + 1], recv.at[seat], {"row": device(t, x)})
            for k, t in enumerate(to)
        )

    def from_seats(buf, send, recv):
        for k in range(1, SEATS):
            src = lax.rem(seat + k, SEATS)
            remote(buf.at[src], buf.at[src], send.at[k], recv.at[src], {"row": device(src, x)}).wait_recv()

    row_pass(keys, cents, scores, peak, total, 4, NT)
    for b in range(NK // 128):
        rows = slice(b * 128, (b + 1) * 128)
        top = peak[rows, :].T
        best = jnp.max(top, axis=0, keepdims=True)
        part = jnp.sum(total[rows, :].T * jnp.exp2(top - best), axis=0, keepdims=True)
        from_list1[lst, 0, b : b + 1, :] = best
        from_list1[lst, 1, b : b + 1, :] = part
    to_list(from_list1, list1_s, list1_r)
    from_list(from_list1, list1_s, list1_r)
    best = tree(jnp.maximum, [from_list1[k, 0] for k in range(N_LIST)])
    whole = tree(jnp.add, [from_list1[k, 1] * jnp.exp2(from_list1[k, 0] - best) for k in range(N_LIST)])
    row1 = -LOG2_KEYS - (best + log2(whole))
    spread(row1, NK // 128, row_pot)

    column_pass(scores, row_pot, stats, 0, 4)
    gather.stage2()
    column_pass(scores, row_pot, stats, 4, NT)
    from_row2[row] = stats[seat]
    to_row(stats, from_row2, row2_s, row2_r)
    from_row(from_row2, row2_s, row2_r)
    best = tree(jnp.maximum, [from_row2[k, 0] for k in range(N_ROW)])
    whole = tree(jnp.add, [from_row2[k, 1] * jnp.exp2(from_row2[k, 0] - best) for k in range(N_ROW)])
    pots[seat] = -LOG2_LISTS - (best + log2(whole))
    to_seats(pots, pot_s, pot_r)
    gather.stage3()
    from_seats(pots, pot_s, pot_r)

    for q in range(SEATS):
        g = jnp.exp2(stats[q, 0] + pots[q])
        gains[q] = g
        for b in range(BLOCKS):
            j = q * BLOCKS + b
            v = j % (W // 128)
            gain[j // (W // 128), :, v * 128 : (v + 1) * 128] = jnp.broadcast_to(g[b : b + 1, :], (8, 128))
    row_sums(scores, gain, total)
    for b in range(NK // 128):
        from_list3[lst, b : b + 1, :] = jnp.sum(total[b * 128 : (b + 1) * 128, :].T, axis=0, keepdims=True)
    to_list(from_list3, list3_s, list3_r)
    from_list(from_list3, list3_s, list3_r)
    delta = -LOG2_KEYS - log2(tree(jnp.add, [from_list3[k] for k in range(N_LIST)]))
    row2 = row1 + delta
    row_all[seat] = row2
    to_seats(row_all, all_s, all_r)
    rowpot_ref[...] = row2 * LN2
    spread(jnp.exp2(delta), NK // 128, row_pot)

    column_sums(scores, row_pot, sums)
    for q in range(SEATS):
        sums[q] = sums[q] * gains[q]
    from_row4[row] = sums[seat]
    to_row(sums, from_row4, row4_s, row4_r)
    gather.arrive()
    from_seats(row_all, all_s, all_r)
    for q in range(SEATS):
        for b in range(NK // 128):
            row_lanes[:, (q * 8 + b) * 128 : (q * 8 + b + 1) * 128] = row_all[q, b : b + 1, :]
    from_row(from_row4, row4_s, row4_r)
    list2 = pots[seat] - LOG2_LISTS - log2(tree(jnp.add, [from_row4[k] for k in range(N_ROW)]))
    pots2[seat] = list2
    to_seats(pots2, pot2_s, pot2_r)
    spread(list2 + LOG2_LISTS, BLOCKS, list_lanes)

    half = LB // 2

    def chunk_at(ch):
        def at(y, x, part, of=core):
            base = pl.multiple_of((y * 2 + of) * SHARE + ch * LB + x * half, half)
            if part is None:
                return new_ref.at[pl.ds(base, half)]
            return new_ref.at[pl.ds(pl.multiple_of(base + part * (half // 2), half // 2), half // 2)]

        return at

    outs = [Gather(chunk_at(ch), out_s.at[ch], out_r.at[ch], y, x, core, done.at[ch]) for ch in range(NCH)]
    side = {"row": device(seat, 1 - x)}
    mine, theirs = pl.multiple_of(x * half, half), pl.multiple_of((1 - x) * half, half)

    def swap(ch):
        return remote(give.at[ch], came.at[ch], twin_s.at[ch], twin_r.at[ch], side)

    def begin_swap(ch):
        give[ch] = acc[ch, pl.ds(theirs, half), :].astype(bf16)
        swap(ch).start()

    def keep(ch):
        return pltpu.make_async_copy(done.at[ch], chunk_at(ch)(y, x, None), here.at[ch])

    def begin(ch):
        swap(ch).wait()
        done[ch] = (acc[ch, pl.ds(mine, half), :] + came[ch].astype(f32)).astype(bf16)
        outs[ch].stage1()
        keep(ch).start()

    def tile(t):
        return keys_all[lax.div(t * KT, NK)]

    def mm1(ch, t):
        c = cents[pl.ds(pl.multiple_of(seat * SHARE + ch * LB, LB), LB), :]
        return lax.dot_general(c, tile(t), NT_DIMS, preferred_element_type=f32)

    def weigh(s_ref, ch, t):
        c = list_lanes[pl.ds(pl.multiple_of(ch * LB, LB), LB), :]
        out = []
        for v in range(KT // 128):
            r = row_lanes[:, pl.ds(pl.multiple_of(t * KT + v * 128, 128), 128)]
            s = s_ref[:, v * 128 : (v + 1) * 128] * SCALE
            out.append(jnp.exp2((s + r) + c).astype(bf16))
        return jnp.concatenate(out, axis=1)

    def mm2(w, t):
        return lax.dot_general(w, tile(t), NN_DIMS, preferred_element_type=f32)

    acc[...] = jnp.zeros(acc.shape, f32)
    sa[...] = mm1(0, 0)

    def step(i, carry):
        ch, t = lax.div(i, STEPS), 2 * lax.rem(i, STEPS)
        nxt = lax.rem(i + 1, NCH * STEPS)
        sb[...] = mm1(ch, t + 1)
        first = mm2(weigh(sa, ch, t), t)
        sa[...] = mm1(lax.div(nxt, STEPS), 2 * lax.rem(nxt, STEPS))
        acc[ch] += first + mm2(weigh(sb, ch, t + 1), t + 1)

        def when(n, *jobs):
            @pl.when(i == n)
            def _():
                for job in jobs:
                    job()

        when(3, lambda: begin_swap(0))
        when(4, lambda: begin(0))
        when(6, lambda: outs[0].stage2())
        when(7, lambda: begin_swap(1))
        when(8, lambda: begin(1), lambda: outs[0].stage3())
        when(10, lambda: outs[1].stage2(), lambda: outs[0].stage4())
        return carry

    lax.fori_loop(0, NCH * STEPS, step, 0)
    begin_swap(2)
    outs[1].stage3()
    from_seats(pots2, pot2_s, pot2_r)
    for q in range(SEATS):
        listpot_ref[q * BLOCKS : (q + 1) * BLOCKS, :] = pots2[q, 0:BLOCKS, :] * LN2
    begin(2)
    outs[1].stage4()
    outs[2].stage2()
    outs[2].stage3()
    outs[2].stage4()
    for ch in range(NCH):
        keep(ch).wait()
        outs[ch].arrive()
        outs[ch].sent()
    gather.sent()
    for copy in sent:
        copy.wait_send()


def local(key_rows, centroids):
    vmem = pl.BlockSpec(memory_space=pltpu.VMEM)
    dma = pltpu.SemaphoreType.DMA
    small = (8, 128)
    new, row_pot, list_pot = pl.pallas_call(
        kernel,
        out_shape=(
            jax.ShapeDtypeStruct((NL, D), bf16),
            jax.ShapeDtypeStruct(small, f32),
            jax.ShapeDtypeStruct((NL // 128, 128), f32),
        ),
        in_specs=[vmem, vmem],
        out_specs=(pl.BlockSpec(memory_space=pl.ANY), vmem, vmem),
        scratch_shapes=[
            pltpu.VMEM((NT, NK, W), f32),
            pltpu.VMEM((NK, 128), f32),
            pltpu.VMEM((NK, 128), f32),
            pltpu.VMEM((NK, 128), f32),
            pltpu.VMEM((NT, 8, W), f32),
            pltpu.VMEM((SEATS, *small), f32),
            pltpu.VMEM((SEATS, 2, *small), f32),
            pltpu.VMEM((SEATS, *small), f32),
            pltpu.VMEM((SEATS, *small), f32),
            pltpu.VMEM((SEATS, *small), f32),
            pltpu.VMEM((N_LIST, 2, *small), f32),
            pltpu.VMEM((N_LIST, *small), f32),
            pltpu.VMEM((N_ROW, 2, *small), f32),
            pltpu.VMEM((N_ROW, *small), f32),
            pltpu.VMEM((SEATS, *small), f32),
            pltpu.VMEM((SEATS, NK, D), bf16),
            pltpu.VMEM((1, SEATS * NK), f32),
            pltpu.VMEM((SHARE, 128), f32),
            pltpu.VMEM((LB, KT), f32),
            pltpu.VMEM((LB, KT), f32),
            pltpu.VMEM((NCH, LB, D), f32),
            pltpu.VMEM((NCH, LB // 2, D), bf16),
            pltpu.VMEM((NCH, LB // 2, D), bf16),
            pltpu.VMEM((NCH, LB // 2, D), bf16),
            dma((N_LIST,)), dma((N_LIST,)), dma((N_LIST,)), dma((N_LIST,)),
            dma((N_ROW,)), dma((N_ROW,)), dma((N_ROW,)), dma((N_ROW,)),
            dma((SEATS,)), dma((SEATS,)), dma((SEATS,)), dma((SEATS,)), dma((SEATS,)), dma((SEATS,)),
            dma((20,)), dma((20,)), dma((NCH,)), dma((NCH,)), dma((NCH, 20)), dma((NCH, 20)), dma((NCH,)),
        ],
        compiler_params=pltpu.CompilerParams(
            collective_id=0, has_side_effects=True, vmem_limit_bytes=60 * 2**20
        ),
        name="sinkhorn",
    )(key_rows, centroids)
    return new, row_pot.reshape(NK), list_pot.reshape(NL)


def solution(mesh):
    return jax.shard_map(
        local,
        mesh=mesh,
        in_specs=(P("row", None), P("list", None)),
        out_specs=(P("list", None), P("row"), P("list")),
        check_vma=False,
    )
```

```python
import math

import jax
import jax.numpy as jnp
from jax import lax
from jax.experimental import pallas as pl
from jax.experimental.pallas import tpu as pltpu
from jax.sharding import PartitionSpec as P

MESH = pl.DeviceIdType.MESH
f32 = jnp.float32
bf16 = jnp.bfloat16
LOG2E = math.log2(math.e)
LN2 = math.log(2.0)

D = 256
SCALE = 2.0 / math.sqrt(D) * LOG2E
NK = 1024
NL = 6144
W = 512
NT = NL // W
N_ROW, N_LIST, SEATS = 16, 8, 8
SHARE = NL // SEATS
BLOCKS = SHARE // 128
LB = 256
NCH = SHARE // LB
KT = 1024
STEPS = SEATS * NK // (2 * KT)
LOG2_KEYS = math.log2(NK * N_ROW)
LOG2_LISTS = math.log2(NL * N_LIST)
NT_DIMS = (((1,), (1,)), ((), ()))
NN_DIMS = (((1,), (0,)), ((), ()))


def tree(op, xs):
    xs = list(xs)
    while len(xs) > 1:
        ys = [op(a, b) for a, b in zip(xs[::2], xs[1::2])]
        if len(xs) % 2:
            ys.append(xs[-1])
        xs = ys
    return xs[0]


def log2(x):
    return jnp.log(x) * LOG2E


def fold(op, x):
    return tree(op, [x[8 * i : 8 * i + 8] for i in range(x.shape[0] // 8)])


def row_pass(keys, cents, scores, peak, total, first, last):
    rb = 32

    def body(i, carry):
        for half in range(2):
            t = 2 * i + half
            lists = pl.ds(pl.multiple_of(t * W, W), W)
            s = lax.dot_general(keys[...], cents[lists, :], NT_DIMS, preferred_element_type=f32) * SCALE
            scores[t] = s
            for b in range(NK // rb):
                rows = slice(b * rb, (b + 1) * rb)
                xs = [s[rows, v * 128 : (v + 1) * 128] for v in range(W // 128)]
                before = peak[rows, :]
                top = jnp.maximum(before, tree(jnp.maximum, xs))
                sums = tree(jnp.add, [jnp.exp2(x - top) for x in xs])
                total[rows, :] = total[rows, :] * jnp.exp2(before - top) + sums
                peak[rows, :] = top
        return carry

    lax.fori_loop(first // 2, last // 2, body, 0)


def column_pass(scores, row_pot, stats, first, last):
    rb = 256

    def body(i, carry):
        for v in range(W // 128):
            lanes = slice(v * 128, (v + 1) * 128)
            tops = []
            for b in range(NK // rb):
                rows = slice(b * rb, (b + 1) * rb)
                x = scores[i, rows, lanes] + row_pot[rows, :]
                scores[i, rows, lanes] = x
                tops.append(fold(jnp.maximum, x))
            top = jnp.max(tree(jnp.maximum, tops), axis=0, keepdims=True)
            sums = []
            for b in range(NK // rb):
                rows = slice(b * rb, (b + 1) * rb)
                e = jnp.exp2(scores[i, rows, lanes] - top)
                scores[i, rows, lanes] = e
                sums.append(fold(jnp.add, e))
            total = jnp.sum(tree(jnp.add, sums), axis=0, keepdims=True)
            j = i * (W // 128) + v
            q, at = lax.div(j, BLOCKS), lax.rem(j, BLOCKS)
            stats[pl.ds(q, 1), 0, pl.ds(at, 1), :] = top[None]
            stats[pl.ds(q, 1), 1, pl.ds(at, 1), :] = total[None]
        return carry

    lax.fori_loop(first, last, body, 0)


def row_sums(scores, gain, total):
    rb, group = 64, 4

    def body(i, carry):
        def at(b):
            return pl.ds(pl.multiple_of(i * rb + 8 * b, 8), 8)

        def inner(c, accs):
            accs = list(accs)
            for t in range(group):
                for v in range(W // 128):
                    lanes = slice(v * 128, (v + 1) * 128)
                    g = gain[c * group + t, :, lanes]
                    for b in range(rb // 8):
                        accs[b] = accs[b] + scores[c * group + t, at(b), lanes] * g
            return tuple(accs)

        zero = jnp.zeros((8, 128), f32)
        accs = lax.fori_loop(0, NT // group, inner, (zero,) * (rb // 8))
        for b in range(rb // 8):
            total[at(b), :] = accs[b]
        return carry

    lax.fori_loop(0, NK // rb, body, 0)


def column_sums(scores, factor, sums):
    rb = 128

    def body(i, carry):
        accs = [[] for _ in range(W // 128)]
        for b in range(NK // rb):
            rows = slice(b * rb, (b + 1) * rb)
            u = factor[rows, :]
            for v in range(W // 128):
                part = fold(jnp.add, scores[i, rows, v * 128 : (v + 1) * 128] * u)
                accs[v] = part if b == 0 else accs[v] + part
        for v in range(W // 128):
            j = i * (W // 128) + v
            q, at = lax.div(j, BLOCKS), lax.rem(j, BLOCKS)
            sums[pl.ds(q, 1), pl.ds(at, 1), :] = jnp.sum(accs[v], axis=0, keepdims=True)[None]
        return carry

    lax.fori_loop(0, NT, body, 0)


def spread(compact, n, out):
    for b in range(n):
        out[b * 128 : (b + 1) * 128, :] = jnp.broadcast_to(compact[b : b + 1, :], (128, 128)).T


def remote(src, dst, send, recv, target):
    return pltpu.make_async_remote_copy(
        src_ref=src, dst_ref=dst, send_sem=send, recv_sem=recv, device_id=target, device_id_type=MESH
    )


class Gather:
    def __init__(self, at, send, recv, y, x, core, own, ring=False):
        self.at, self.send, self.recv = at, send, recv
        self.y, self.x, self.core, self.own, self.ring = y, x, core, own, ring

        def device(dy, flip, of=core):
            return {"row": (lax.rem(y + dy + 4, 4) * 2 + (1 - x if flip else x)) * 2 + of}

        up, down, side = device(1, False), device(-1, False), device(0, True)
        self.other = device(0, False, 1 - core)
        self.moves = [
            (up, (0, False), (-1, False), None),
            (down, (0, False), (1, False), None),
            (up, (-1, False), (-2, False), 0),
            (down, (1, False), (2, False), 1),
            (side, (0, False), (0, True), None),
            (up, (0, True), (-1, True), None),
            (down, (0, True), (1, True), None),
            (side, (-2, False), (2, True), 0),
            (side, (2, False), (2, True), 1),
        ]
        self.used = range(4) if ring else range(9)

    def place(self, block, part, *of):
        dy, flip = block
        return self.at(lax.rem(self.y + dy + 4, 4), 1 - self.x if flip else self.x, part, *of)

    def source(self, block, part):
        return self.own if block == (0, False) else self.place(block, part)

    def copy(self, m):
        target, sent, _, part = self.moves[m]
        return remote(self.source(sent, part), self.place(sent, part), self.send.at[m], self.recv.at[m], target)

    def arrival(self, m):
        target, _, came, part = self.moves[m]
        place = self.place(came, part)
        return remote(place, place, self.send.at[m], self.recv.at[m], target)

    def brought(self, m):
        return ((0, False), None) if m == 9 else self.moves[m][2:]

    def hand(self, m):
        block, part = self.brought(m)
        return remote(
            self.source(block, part), self.place(block, part), self.send.at[10 + m], self.recv.at[10 + m], self.other
        )

    def handed(self, m):
        block, part = self.brought(m)
        place = self.place(block, part, 1 - self.core)
        return remote(place, place, self.send.at[10 + m], self.recv.at[10 + m], self.other)

    def take(self, m, *sends):
        if m in self.used:
            self.arrival(m).wait_recv()
            for n in sends:
                if n in self.used:
                    self.copy(n).start()
            self.hand(m).start()

    def stage1(self):
        for m in (0, 1, 4):
            if m in self.used:
                self.copy(m).start()
        self.hand(9).start()

    def stage2(self):
        self.take(0, 2)
        self.take(1, 3)
        self.take(4, 5, 6)

    def stage3(self):
        self.take(2, 7)
        self.take(3, 8)

    def stage4(self):
        for m in (5, 6, 7, 8):
            self.take(m)

    def arrive(self):
        for m in (*self.used, 9):
            self.handed(m).wait_recv()

    def sent(self):
        for m in self.used:
            self.copy(m).wait_send()
        for m in (*self.used, 9):
            self.hand(m).wait_send()


def kernel(
    keys, cents, new_ref, rowpot_ref, listpot_ref,
    scores, peak, total, row_pot, gain, gains, stats, sums, pots, pots2, from_list1, from_list3, from_row2, from_row4,
    row_all, keys_all, row_lanes, list_lanes, sa, sb, wa, wb, acc, give, came, done,
    list1_s, list1_r, list3_s, list3_r, row2_s, row2_r, row4_s, row4_r, pot_s, pot_r, pot2_s, pot2_r, all_s, all_r,
    keys_s, keys_r, twin_s, twin_r, out_s, out_r, here,
):
    row, lst = lax.axis_index("row"), lax.axis_index("list")
    core, x, y = lax.rem(row, 2), lax.rem(lax.div(row, 2), 2), lax.div(row, 4)
    seat = y * 2 + core

    def device(at, x):
        return (lax.div(at, 2) * 2 + x) * 2 + lax.rem(at, 2)

    def seat_of(device):
        return lax.div(device, 4) * 2 + lax.rem(device, 2)

    barrier = pltpu.get_barrier_semaphore()
    for k in range(1, N_ROW):
        pl.semaphore_signal(barrier, inc=1, device_id={"row": lax.rem(row + k, N_ROW)}, device_id_type=MESH)
    for k in range(1, N_LIST):
        pl.semaphore_signal(barrier, inc=1, device_id={"list": lax.rem(lst + k, N_LIST)}, device_id_type=MESH)
    stats[...] = jnp.zeros(stats.shape, f32)
    sums[...] = jnp.zeros(sums.shape, f32)
    peak[...] = jnp.full(peak.shape, -1e30, f32)
    total[...] = jnp.zeros(total.shape, f32)
    keys_all[seat] = keys[...]
    row_pass(keys, cents, scores, peak, total, 0, 4)
    pl.semaphore_wait(barrier, N_ROW + N_LIST - 2)

    def keys_at(y, x, part, of=core):
        at = y * 2 + of
        return keys_all.at[at] if part is None else keys_all.at[at, pl.ds(part * (NK // 2), NK // 2)]

    gather = Gather(keys_at, keys_s, keys_r, y, x, core, keys, ring=True)
    gather.stage1()
    sent = []

    def start(copies):
        for copy in copies:
            copy.start()
            sent.append(copy)

    def to_list(buf, send, recv):
        start(
            remote(buf.at[lst], buf.at[lst], send.at[k], recv.at[lst], {"list": lax.rem(lst + k, N_LIST)})
            for k in range(1, N_LIST)
        )

    def from_list(buf, send, recv):
        for k in range(1, N_LIST):
            src = lax.rem(lst + k, N_LIST)
            remote(buf.at[src], buf.at[src], send.at[k], recv.at[src], {"list": src}).wait_recv()

    def to_row(src_of, buf, send, recv):
        to = [lax.rem(row + k, N_ROW) for k in range(1, N_ROW)]
        start(
            remote(src_of.at[seat_of(t)], buf.at[row], send.at[k + 1], recv.at[row], {"row": t})
            for k, t in enumerate(to)
        )

    def from_row(buf, send, recv):
        for k in range(1, N_ROW):
            src = lax.rem(row + k, N_ROW)
            remote(buf.at[src], buf.at[src], send.at[k], recv.at[src], {"row": src}).wait_recv()

    def to_seats(buf, send, recv):
        to = [lax.rem(seat + k, SEATS) for k in range(1, SEATS)]
        start(
            remote(buf.at[seat], buf.at[seat], send.at[k + 1], recv.at[seat], {"row": device(t, x)})
            for k, t in enumerate(to)
        )

    def from_seats(buf, send, recv):
        for k in range(1, SEATS):
            src = lax.rem(seat + k, SEATS)
            remote(buf.at[src], buf.at[src], send.at[k], recv.at[src], {"row": device(src, x)}).wait_recv()

    row_pass(keys, cents, scores, peak, total, 4, NT)
    for b in range(NK // 128):
        rows = slice(b * 128, (b + 1) * 128)
        top = peak[rows, :].T
        best = jnp.max(top, axis=0, keepdims=True)
        part = jnp.sum(total[rows, :].T * jnp.exp2(top - best), axis=0, keepdims=True)
        from_list1[lst, 0, b : b + 1, :] = best
        from_list1[lst, 1, b : b + 1, :] = part
    to_list(from_list1, list1_s, list1_r)
    from_list(from_list1, list1_s, list1_r)
    best = tree(jnp.maximum, [from_list1[k, 0] for k in range(N_LIST)])
    whole = tree(jnp.add, [from_list1[k, 1] * jnp.exp2(from_list1[k, 0] - best) for k in range(N_LIST)])
    row1 = -LOG2_KEYS - (best + log2(whole))
    spread(row1, NK // 128, row_pot)

    column_pass(scores, row_pot, stats, 0, 4)
    gather.stage2()
    column_pass(scores, row_pot, stats, 4, NT)
    from_row2[row] = stats[seat]
    to_row(stats, from_row2, row2_s, row2_r)
    from_row(from_row2, row2_s, row2_r)
    best = tree(jnp.maximum, [from_row2[k, 0] for k in range(N_ROW)])
    whole = tree(jnp.add, [from_row2[k, 1] * jnp.exp2(from_row2[k, 0] - best) for k in range(N_ROW)])
    pots[seat] = -LOG2_LISTS - (best + log2(whole))
    to_seats(pots, pot_s, pot_r)
    gather.stage3()
    from_seats(pots, pot_s, pot_r)

    for q in range(SEATS):
        g = jnp.exp2(stats[q, 0] + pots[q])
        gains[q] = g
        for b in range(BLOCKS):
            j = q * BLOCKS + b
            v = j % (W // 128)
            gain[j // (W // 128), :, v * 128 : (v + 1) * 128] = jnp.broadcast_to(g[b : b + 1, :], (8, 128))
    row_sums(scores, gain, total)
    for b in range(NK // 128):
        from_list3[lst, b : b + 1, :] = jnp.sum(total[b * 128 : (b + 1) * 128, :].T, axis=0, keepdims=True)
    to_list(from_list3, list3_s, list3_r)
    from_list(from_list3, list3_s, list3_r)
    delta = -LOG2_KEYS - log2(tree(jnp.add, [from_list3[k] for k in range(N_LIST)]))
    row2 = row1 + delta
    row_all[seat] = row2
    to_seats(row_all, all_s, all_r)
    rowpot_ref[...] = row2 * LN2
    spread(jnp.exp2(delta), NK // 128, row_pot)

    column_sums(scores, row_pot, sums)
    for q in range(SEATS):
        sums[q] = sums[q] * gains[q]
    from_row4[row] = sums[seat]
    to_row(sums, from_row4, row4_s, row4_r)
    gather.arrive()
    from_seats(row_all, all_s, all_r)
    for q in range(SEATS):
        for b in range(NK // 128):
            row_lanes[:, (q * 8 + b) * 128 : (q * 8 + b + 1) * 128] = row_all[q, b : b + 1, :]
    from_row(from_row4, row4_s, row4_r)
    list2 = pots[seat] - LOG2_LISTS - log2(tree(jnp.add, [from_row4[k] for k in range(N_ROW)]))
    pots2[seat] = list2
    to_seats(pots2, pot2_s, pot2_r)
    spread(list2 + LOG2_LISTS, BLOCKS, list_lanes)

    half = LB // 2

    def chunk_at(ch):
        def at(y, x, part, of=core):
            base = pl.multiple_of((y * 2 + of) * SHARE + ch * LB + x * half, half)
            if part is None:
                return new_ref.at[pl.ds(base, half)]
            return new_ref.at[pl.ds(pl.multiple_of(base + part * (half // 2), half // 2), half // 2)]

        return at

    outs = [Gather(chunk_at(ch), out_s.at[ch], out_r.at[ch], y, x, core, done.at[ch]) for ch in range(NCH)]
    side = {"row": device(seat, 1 - x)}
    mine, theirs = pl.multiple_of(x * half, half), pl.multiple_of((1 - x) * half, half)

    def swap(ch):
        return remote(give.at[ch], came.at[ch], twin_s.at[ch], twin_r.at[ch], side)

    def begin_swap(ch):
        give[ch] = acc[ch, pl.ds(theirs, half), :].astype(bf16)
        swap(ch).start()

    def keep(ch):
        return pltpu.make_async_copy(done.at[ch], chunk_at(ch)(y, x, None), here.at[ch])

    def begin(ch):
        swap(ch).wait()
        done[ch] = (acc[ch, pl.ds(mine, half), :] + came[ch].astype(f32)).astype(bf16)
        outs[ch].stage1()
        keep(ch).start()

    def tile(t):
        return keys_all[lax.div(t * KT, NK)]

    def mm1(ch, t):
        c = cents[pl.ds(pl.multiple_of(seat * SHARE + ch * LB, LB), LB), :]
        return lax.dot_general(c, tile(t), NT_DIMS, preferred_element_type=f32)

    def mm2(w_ref, t):
        return lax.dot_general(w_ref[...], tile(t), NN_DIMS, preferred_element_type=f32)

    def weigh(s_ref, w_ref, ch, t):
        c = list_lanes[pl.ds(pl.multiple_of(ch * LB, LB), LB), :]
        for v in range(KT // 128):
            lanes = slice(v * 128, (v + 1) * 128)
            r = row_lanes[:, pl.ds(pl.multiple_of(t * KT + v * 128, 128), 128)]
            w_ref[:, lanes] = jnp.exp2((s_ref[:, lanes] * SCALE + r) + c).astype(bf16)

    acc[...] = jnp.zeros(acc.shape, f32)
    wb[...] = jnp.zeros(wb.shape, bf16)
    sa[...] = mm1(0, 0)

    def step(i, carry):
        ch, t = lax.div(i, STEPS), 2 * lax.rem(i, STEPS)
        nxt, prv = lax.rem(i + 1, NCH * STEPS), lax.rem(i + NCH * STEPS - 1, NCH * STEPS)
        before = mm2(wb, 2 * lax.rem(prv, STEPS) + 1)
        sb[...] = mm1(ch, t + 1)
        weigh(sa, wa, ch, t)
        acc[lax.div(prv, STEPS)] += before
        now = mm2(wa, t)
        sa[...] = mm1(lax.div(nxt, STEPS), 2 * lax.rem(nxt, STEPS))
        weigh(sb, wb, ch, t + 1)
        acc[ch] += now

        def when(n, *jobs):
            @pl.when(i == n)
            def _():
                for job in jobs:
                    job()

        when(STEPS, lambda: begin_swap(0))
        when(2 * STEPS - 1, lambda: begin(0))
        when(2 * STEPS, lambda: begin_swap(1))
        when(3 * STEPS - 1, lambda: begin(1), outs[0].stage2)
        return carry

    lax.fori_loop(0, NCH * STEPS, step, 0)
    acc[NCH - 1] += mm2(wb, SEATS * NK // KT - 1)
    begin_swap(2)
    outs[0].stage3()
    outs[1].stage2()
    from_seats(pots2, pot2_s, pot2_r)
    for q in range(SEATS):
        listpot_ref[q * BLOCKS : (q + 1) * BLOCKS, :] = pots2[q, 0:BLOCKS, :] * LN2
    begin(2)
    outs[1].stage3()
    outs[0].stage4()
    outs[2].stage2()
    outs[1].stage4()
    outs[2].stage3()
    outs[2].stage4()
    for ch in range(NCH):
        keep(ch).wait()
        outs[ch].arrive()
        outs[ch].sent()
    gather.sent()
    for copy in sent:
        copy.wait_send()


def local(key_rows, centroids):
    vmem = pl.BlockSpec(memory_space=pltpu.VMEM)
    dma = pltpu.SemaphoreType.DMA
    small = (8, 128)
    new, row_pot, list_pot = pl.pallas_call(
        kernel,
        out_shape=(
            pltpu.VMEM((NL, D), bf16),
            jax.ShapeDtypeStruct(small, f32),
            jax.ShapeDtypeStruct((NL // 128, 128), f32),
        ),
        in_specs=[vmem, vmem],
        out_specs=(pl.BlockSpec(memory_space=pl.ANY), vmem, vmem),
        scratch_shapes=[
            pltpu.VMEM((NT, NK, W), f32),
            pltpu.VMEM((NK, 128), f32),
            pltpu.VMEM((NK, 128), f32),
            pltpu.VMEM((NK, 128), f32),
            pltpu.VMEM((NT, 8, W), f32),
            pltpu.VMEM((SEATS, *small), f32),
            pltpu.VMEM((SEATS, 2, *small), f32),
            pltpu.VMEM((SEATS, *small), f32),
            pltpu.VMEM((SEATS, *small), f32),
            pltpu.VMEM((SEATS, *small), f32),
            pltpu.VMEM((N_LIST, 2, *small), f32),
            pltpu.VMEM((N_LIST, *small), f32),
            pltpu.VMEM((N_ROW, 2, *small), f32),
            pltpu.VMEM((N_ROW, *small), f32),
            pltpu.VMEM((SEATS, *small), f32),
            pltpu.VMEM((SEATS, NK, D), bf16),
            pltpu.VMEM((1, SEATS * NK), f32),
            pltpu.VMEM((SHARE, 128), f32),
            pltpu.VMEM((LB, KT), f32),
            pltpu.VMEM((LB, KT), f32),
            pltpu.VMEM((LB, KT), bf16),
            pltpu.VMEM((LB, KT), bf16),
            pltpu.VMEM((NCH, LB, D), f32),
            pltpu.VMEM((NCH, LB // 2, D), bf16),
            pltpu.VMEM((NCH, LB // 2, D), bf16),
            pltpu.VMEM((NCH, LB // 2, D), bf16),
            dma((N_LIST,)), dma((N_LIST,)), dma((N_LIST,)), dma((N_LIST,)),
            dma((N_ROW,)), dma((N_ROW,)), dma((N_ROW,)), dma((N_ROW,)),
            dma((SEATS,)), dma((SEATS,)), dma((SEATS,)), dma((SEATS,)), dma((SEATS,)), dma((SEATS,)),
            dma((20,)), dma((20,)), dma((NCH,)), dma((NCH,)), dma((NCH, 20)), dma((NCH, 20)), dma((NCH,)),
        ],
        compiler_params=pltpu.CompilerParams(
            collective_id=0, has_side_effects=True, vmem_limit_bytes=44 * 2**20
        ),
        name="sinkhorn",
    )(key_rows, centroids)
    return new, row_pot.reshape(NK), list_pot.reshape(NL)


def solution(mesh):
    return jax.shard_map(
        local,
        mesh=mesh,
        in_specs=(P("row", None), P("list", None)),
        out_specs=(P("list", None), P("row"), P("list")),
        check_vma=False,
    )
```

```python
import math

import jax
import jax.numpy as jnp
from jax import lax
from jax.experimental import pallas as pl
from jax.experimental.pallas import tpu as pltpu
from jax.sharding import PartitionSpec as P

MESH = pl.DeviceIdType.MESH
f32 = jnp.float32
bf16 = jnp.bfloat16
LOG2E = math.log2(math.e)
LN2 = math.log(2.0)

D = 256
SCALE = 2.0 / math.sqrt(D) * LOG2E
NK = 1024
NL = 6144
W = 512
NT = NL // W
HALF = NK // 2
N_ROW, N_LIST, SEATS = 16, 8, 8
SHARE = NL // SEATS
BLOCKS = SHARE // 128
LB = SHARE // 2
PIECE = 128
NCH = LB // PIECE
VMEM = 243 * 2**18
KT = 1024
STEPS = SEATS * NK // (2 * KT)
LOG2_KEYS = math.log2(NK * N_ROW)
LOG2_LISTS = math.log2(NL * N_LIST)
NT_DIMS = (((1,), (1,)), ((), ()))
NN_DIMS = (((1,), (0,)), ((), ()))


def tree(op, xs):
    xs = list(xs)
    while len(xs) > 1:
        ys = [op(a, b) for a, b in zip(xs[::2], xs[1::2])]
        if len(xs) % 2:
            ys.append(xs[-1])
        xs = ys
    return xs[0]


def log2(x):
    return jnp.log(x) * LOG2E


def fold(op, x):
    return tree(op, [x[8 * i : 8 * i + 8] for i in range(x.shape[0] // 8)])


def score_tile(keys, cents, scores, peak, i, half, part):
    rb = 32
    lists = pl.ds(pl.multiple_of((2 * i + half) * W, W), W)
    mine = keys[part * HALF : (part + 1) * HALF, :]
    s = lax.dot_general(mine, cents[lists, :], NT_DIMS, preferred_element_type=f32) * SCALE
    scores[i, half, part] = s
    for b in range(HALF // rb):
        rows = slice(part * HALF + b * rb, part * HALF + (b + 1) * rb)
        xs = [s[b * rb : (b + 1) * rb, v * 128 : (v + 1) * 128] for v in range(W // 128)]
        peak[rows, :] = jnp.maximum(peak[rows, :], tree(jnp.maximum, xs))


def sum_tile(scores, peak, total, i, half, part):
    rb = 32
    for b in range(HALF // rb):
        rows = slice(part * HALF + b * rb, part * HALF + (b + 1) * rb)
        top = peak[rows, :]
        xs = [scores[i, half, part, b * rb : (b + 1) * rb, v * 128 : (v + 1) * 128] for v in range(W // 128)]
        total[rows, :] += tree(jnp.add, [jnp.exp2(x - top) for x in xs])


def row_pass(work):
    def body(i, carry):
        for half in range(2):
            for step in work:
                step(i, half)
        return carry

    lax.fori_loop(0, NT // 2, body, 0)


def column_pass(scores, row_pot, stats, part, first, last):
    rb = 64
    columns = [(half, v) for half in range(2) for v in range(W // 128)]

    def body(i, carry):
        def at(n, b):
            half, v = columns[n]
            return i, half, part, slice(b * rb, (b + 1) * rb), slice(v * 128, (v + 1) * 128)

        top = None
        for n in range(len(columns) + 1):
            peaks = sums = None
            for b in range(HALF // rb):
                if n < len(columns):
                    x = scores[at(n, b)] + row_pot[part * HALF + b * rb : part * HALF + (b + 1) * rb, :]
                    scores[at(n, b)] = x
                    x = fold(jnp.maximum, x)
                    peaks = x if b == 0 else jnp.maximum(peaks, x)
                if n > 0:
                    e = jnp.exp2(scores[at(n - 1, b)] - top)
                    scores[at(n - 1, b)] = e
                    e = fold(jnp.add, e)
                    sums = e if b == 0 else sums + e
            if n > 0:
                j = i * len(columns) + n - 1
                q, row = lax.div(j, BLOCKS), lax.rem(j, BLOCKS)
                stats[part, pl.ds(q, 1), 0, pl.ds(row, 1), :] = top[None]
                stats[part, pl.ds(q, 1), 1, pl.ds(row, 1), :] = jnp.sum(sums, axis=0, keepdims=True)[None]
            if n < len(columns):
                top = jnp.max(peaks, axis=0, keepdims=True)
        return carry

    lax.fori_loop(first, last, body, 0)


def row_sums(scores, gain, total, part):
    rb, group = 64, 4

    def body(i, carry):
        def at(b):
            return pl.ds(pl.multiple_of(i * rb + 8 * b, 8), 8)

        def out(b):
            return pl.ds(pl.multiple_of(part * HALF + i * rb + 8 * b, 8), 8)

        def inner(c, accs):
            accs = list(accs)
            for t in range(group):
                for v in range(W // 128):
                    lanes = slice(v * 128, (v + 1) * 128)
                    g = gain[part, c * group + t, :, lanes]
                    for b in range(rb // 8):
                        accs[b] = accs[b] + scores[c * (group // 2) + t // 2, t % 2, part, at(b), lanes] * g
            return tuple(accs)

        zero = jnp.zeros((8, 128), f32)
        accs = lax.fori_loop(0, NT // group, inner, (zero,) * (rb // 8))
        for b in range(rb // 8):
            total[out(b), :] = accs[b]
        return carry

    lax.fori_loop(0, HALF // rb, body, 0)


def spread(compact, n, out, first=0):
    for b in range(n):
        out[first + b * 128 : first + (b + 1) * 128, :] = jnp.broadcast_to(compact[b : b + 1, :], (128, 128)).T


def remote(src, dst, send, recv, target):
    return pltpu.make_async_remote_copy(
        src_ref=src, dst_ref=dst, send_sem=send, recv_sem=recv, device_id=target, device_id_type=MESH
    )


class Gather:
    def __init__(self, at, send, recv, y, x, core, own, ring=False):
        self.at, self.send, self.recv = at, send, recv
        self.y, self.x, self.core, self.own, self.ring = y, x, core, own, ring

        def device(dy, flip, of=core):
            return {"row": (lax.rem(y + dy + 4, 4) * 2 + (1 - x if flip else x)) * 2 + of}

        up, down, side = device(1, False), device(-1, False), device(0, True)
        self.other = device(0, False, 1 - core)
        self.moves = [
            (up, (0, False), (-1, False), None),
            (down, (0, False), (1, False), None),
            (up, (-1, False), (-2, False), 0),
            (down, (1, False), (2, False), 1),
            (side, (0, False), (0, True), None),
            (up, (0, True), (-1, True), None),
            (down, (0, True), (1, True), None),
            (side, (-2, False), (2, True), 0),
            (side, (2, False), (2, True), 1),
        ]
        self.used = range(4) if ring else range(9)

    def place(self, block, part, *of):
        dy, flip = block
        return self.at(lax.rem(self.y + dy + 4, 4), 1 - self.x if flip else self.x, part, *of)

    def source(self, block, part):
        return self.own if block == (0, False) else self.place(block, part)

    def copy(self, m):
        target, sent, _, part = self.moves[m]
        return remote(self.source(sent, part), self.place(sent, part), self.send.at[m], self.recv.at[m], target)

    def arrival(self, m):
        target, _, came, part = self.moves[m]
        place = self.place(came, part)
        return remote(place, place, self.send.at[m], self.recv.at[m], target)

    def brought(self, m):
        return ((0, False), None) if m == 9 else self.moves[m][2:]

    def hand(self, m):
        block, part = self.brought(m)
        return remote(
            self.source(block, part), self.place(block, part), self.send.at[10 + m], self.recv.at[10 + m], self.other
        )

    def handed(self, m):
        block, part = self.brought(m)
        place = self.place(block, part, 1 - self.core)
        return remote(place, place, self.send.at[10 + m], self.recv.at[10 + m], self.other)

    def take(self, m, *sends):
        if m in self.used:
            self.arrival(m).wait_recv()
            for n in sends:
                if n in self.used:
                    self.copy(n).start()
            self.hand(m).start()

    def stage1(self):
        for m in (0, 1, 4):
            if m in self.used:
                self.copy(m).start()
        self.hand(9).start()

    def stage2(self):
        self.take(0, 2)
        self.take(1, 3)
        self.take(4, 5, 6)

    def stage3(self):
        self.take(2, 7)
        self.take(3, 8)

    def stage4(self):
        for m in (5, 6, 7, 8):
            self.take(m)

    def arrive(self):
        for m in (*self.used, 9):
            self.handed(m).wait_recv()

    def sent(self):
        for m in self.used:
            self.copy(m).wait_send()
        for m in (*self.used, 9):
            self.hand(m).wait_send()


def kernel(
    keys_hbm, cents_hbm, new_ref, rowpot_ref, listpot_ref,
    keys, cents, load, scores, peak, total, row_pot, row1, gain, stats, both, pots, pots2, from_list1, from_list3, from_row2,
    row_all, keys_all, row_lanes, list_lanes, sa, sb, wa, wb, acc, give, came, done, tsum, tmine, tcame,
    list1_s, list1_r, list3_s, list3_r, row2_s, row2_r, tsum_s, tsum_r, pot_s, pot_r, pot2_s, pot2_r, all_s, all_r,
    keys_s, keys_r, twin_s, twin_r, out_s, out_r, here,
):
    row, lst = lax.axis_index("row"), lax.axis_index("list")
    core, x, y = lax.rem(row, 2), lax.rem(lax.div(row, 2), 2), lax.div(row, 4)
    seat = y * 2 + core

    def device(at, x):
        return (lax.div(at, 2) * 2 + x) * 2 + lax.rem(at, 2)

    def seat_of(device):
        return lax.div(device, 4) * 2 + lax.rem(device, 2)

    barrier = pltpu.get_barrier_semaphore()
    for k in range(1, N_ROW):
        pl.semaphore_signal(barrier, inc=1, device_id={"row": lax.rem(row + k, N_ROW)}, device_id_type=MESH)
    for k in range(1, N_LIST):
        pl.semaphore_signal(barrier, inc=1, device_id={"list": lax.rem(lst + k, N_LIST)}, device_id_type=MESH)
    stats[...] = jnp.ones(stats.shape, f32)
    tmine[...] = jnp.zeros(tmine.shape, f32)
    pots2[...] = jnp.zeros(pots2.shape, f32)
    peak[...] = jnp.full(peak.shape, -1e30, f32)
    total[...] = jnp.zeros(total.shape, f32)
    loads = [
        pltpu.make_async_copy(keys_hbm, keys, load.at[0]),
        pltpu.make_async_copy(cents_hbm, cents, load.at[1]),
    ]
    for copy in loads:
        copy.start()

    def score(part):
        return lambda i, half: score_tile(keys, cents, scores, peak, i, half, part)

    def add(part):
        return lambda i, half: sum_tile(scores, peak, total, i, half, part)

    for copy in loads:
        copy.wait()
    keys_all[seat] = keys[...]
    row_pass([score(0)])
    row_pass([score(1), add(0)])
    pl.semaphore_wait(barrier, N_ROW + N_LIST - 2)

    def keys_at(y, x, part, of=core):
        at = y * 2 + of
        return keys_all.at[at] if part is None else keys_all.at[at, pl.ds(part * (NK // 2), NK // 2)]

    gather = Gather(keys_at, keys_s, keys_r, y, x, core, keys, ring=True)
    gather.stage1()
    sent = []

    def start(copies):
        for copy in copies:
            copy.start()
            sent.append(copy)

    def to_list(buf, send, recv):
        start(
            remote(buf.at[lst], buf.at[lst], send.at[k], recv.at[lst], {"list": lax.rem(lst + k, N_LIST)})
            for k in range(1, N_LIST)
        )

    def from_list(buf, send, recv):
        for k in range(1, N_LIST):
            src = lax.rem(lst + k, N_LIST)
            remote(buf.at[src], buf.at[src], send.at[k], recv.at[src], {"list": src}).wait_recv()

    def to_row(src_of, buf, send, recv):
        to = [lax.rem(row + k, N_ROW) for k in range(1, N_ROW)]
        start(
            remote(src_of.at[seat_of(t)], buf.at[row], send.at[k + 1], recv.at[row], {"row": t})
            for k, t in enumerate(to)
        )

    def from_row(buf, send, recv):
        for k in range(1, N_ROW):
            src = lax.rem(row + k, N_ROW)
            remote(buf.at[src], buf.at[src], send.at[k], recv.at[src], {"row": src}).wait_recv()

    def to_seats(buf, send, recv):
        to = [lax.rem(seat + k, SEATS) for k in range(1, SEATS)]
        start(
            remote(buf.at[seat], buf.at[seat], send.at[k + 1], recv.at[seat], {"row": device(t, x)})
            for k, t in enumerate(to)
        )

    def from_seats(buf, send, recv):
        for k in range(1, SEATS):
            src = lax.rem(seat + k, SEATS)
            remote(buf.at[src], buf.at[src], send.at[k], recv.at[src], {"row": device(src, x)}).wait_recv()

    n = HALF // 128

    def tell(part):
        for b in range(n):
            rows = slice(part * HALF + b * 128, part * HALF + (b + 1) * 128)
            top = peak[rows, :].T
            best = jnp.max(top, axis=0, keepdims=True)
            from_list1[part, lst, b : b + 1, :] = best
            from_list1[part, lst, n + b : n + b + 1, :] = jnp.sum(
                total[rows, :].T * jnp.exp2(top - best), axis=0, keepdims=True
            )
        to_list(from_list1.at[part], list1_s.at[part], list1_r.at[part])

    def learn(part):
        from_list(from_list1.at[part], list1_s.at[part], list1_r.at[part])
        best = tree(jnp.maximum, [from_list1[part, k, 0:n] for k in range(N_LIST)])
        whole = tree(
            jnp.add, [from_list1[part, k, n : 2 * n] * jnp.exp2(from_list1[part, k, 0:n] - best) for k in range(N_LIST)]
        )
        row1[part * n : (part + 1) * n, :] = -LOG2_KEYS - (best + log2(whole))
        spread(row1[part * n : (part + 1) * n, :], n, row_pot, part * HALF)

    tell(0)
    row_pass([add(1)])
    tell(1)

    learn(0)
    column_pass(scores, row_pot, stats, 0, 0, NT // 2)
    learn(1)
    column_pass(scores, row_pot, stats, 1, 0, NT // 2)
    for q in range(SEATS):
        best = jnp.maximum(stats[0, q, 0], stats[1, q, 0])
        both[q] = best + log2(tree(jnp.add, [stats[p, q, 1] * jnp.exp2(stats[p, q, 0] - best) for p in range(2)]))
    from_row2[row] = both[seat]
    to_row(both, from_row2, row2_s, row2_r)
    from_row(from_row2, row2_s, row2_r)
    best = tree(jnp.maximum, [from_row2[k] for k in range(N_ROW)])
    whole = tree(jnp.add, [jnp.exp2(from_row2[k] - best) for k in range(N_ROW)])
    pots[seat] = -LOG2_LISTS - (best + log2(whole))
    to_seats(pots, pot_s, pot_r)
    from_seats(pots, pot_s, pot_r)
    gather.stage2()

    for q in range(SEATS):
        for p in range(2):
            g = jnp.exp2(stats[p, q, 0] + pots[q])
            for b in range(BLOCKS):
                j = q * BLOCKS + b
                v = j % (W // 128)
                gain[p, j // (W // 128), :, v * 128 : (v + 1) * 128] = jnp.broadcast_to(g[b : b + 1, :], (8, 128))
    row_sums(scores, gain, total, 0)
    row_sums(scores, gain, total, 1)
    for b in range(NK // 128):
        from_list3[lst, b : b + 1, :] = jnp.sum(total[b * 128 : (b + 1) * 128, :].T, axis=0, keepdims=True)
    to_list(from_list3, list3_s, list3_r)
    from_list(from_list3, list3_s, list3_r)
    delta = -LOG2_KEYS - log2(tree(jnp.add, [from_list3[k] for k in range(N_LIST)]))
    row2 = row1[...] + delta
    row_all[seat] = row2
    to_seats(row_all, all_s, all_r)
    rowpot_ref[...] = row2 * LN2
    spread(pots[seat] + LOG2_LISTS, BLOCKS, list_lanes)
    acc[...] = jnp.zeros(acc.shape, f32)
    tsum[...] = jnp.zeros(tsum.shape, f32)
    gather.stage3()

    def base(block):
        return (block * x + (1 - block) * (1 - x)) * LB

    def piece_at(ch):
        def at(y, x, part, of=core):
            first = pl.multiple_of((y * 2 + of) * SHARE + x * LB + ch * PIECE, PIECE)
            if part is None:
                return new_ref.at[pl.ds(first, PIECE)]
            return new_ref.at[pl.ds(pl.multiple_of(first + part * (PIECE // 2), PIECE // 2), PIECE // 2)]

        return at

    outs = [Gather(piece_at(ch), out_s.at[ch], out_r.at[ch], y, x, core, done.at[ch]) for ch in range(NCH)]
    side = {"row": device(seat, 1 - x)}

    def swap(ch):
        return remote(give.at[ch], came.at[ch], twin_s.at[ch], twin_r.at[ch], side)

    def swap_sums(block):
        return remote(tmine.at[block], tcame.at[block], tsum_s.at[block], tsum_r.at[block], side)

    def sums(block):
        for b in range(NCH):
            rows = slice(b * 128, (b + 1) * 128)
            tmine[block, b : b + 1, :] = jnp.sum(tsum[block, rows, :].T, axis=0, keepdims=True)
        swap_sums(block).start()

    def hand_over():
        for ch in range(NCH):
            give[ch] = acc[0, ch * PIECE : (ch + 1) * PIECE, :].astype(bf16)
            swap(ch).start()
        sums(0)

    def keep(ch):
        return pltpu.make_async_copy(done.at[ch], piece_at(ch)(y, x, None), here.at[ch])

    def begin(ch):
        whole = tmine[1, ch : ch + 1, :] + tcame[0, ch : ch + 1, :]
        scale = jnp.broadcast_to(1.0 / whole, (PIECE, 128)).T
        swap(ch).wait()
        for v in range(D // 128):
            lanes = slice(v * 128, (v + 1) * 128)
            summed = acc[1, ch * PIECE : (ch + 1) * PIECE, lanes] + came[ch, :, lanes].astype(f32)
            done[ch, :, lanes] = (summed * scale).astype(bf16)
        outs[ch].stage1()
        keep(ch).start()

    def update(block, other):
        for b in range(NCH):
            at = pl.ds((block * x + (1 - block) * (1 - x)) * NCH + b, 1)
            whole = tmine[block, b : b + 1, :] + tcame[other, b : b + 1, :]
            pots2[seat, at, :] = pots[seat, at, :] - log2(whole)

    def tile(t):
        return keys_all[lax.div(t * KT, NK)]

    def mm1(block, t):
        c = cents[pl.ds(pl.multiple_of(seat * SHARE + base(block), LB), LB), :]
        return lax.dot_general(c, tile(t), NT_DIMS, preferred_element_type=f32)

    def mm2(w_ref, t):
        return lax.dot_general(w_ref[...], tile(t), NN_DIMS, preferred_element_type=f32)

    def weigh(s_ref, w_ref, block, t):
        c = list_lanes[pl.ds(pl.multiple_of(base(block), LB), LB), :]
        parts = []
        for v in range(KT // 128):
            lanes = slice(v * 128, (v + 1) * 128)
            r = row_lanes[:, pl.ds(pl.multiple_of(t * KT + v * 128, 128), 128)]
            e = jnp.exp2((s_ref[:, lanes] * SCALE + r) + c)
            w_ref[:, lanes] = e.astype(bf16)
            parts.append(e)
        tsum[block] += tree(jnp.add, parts)

    wb[...] = jnp.zeros(wb.shape, bf16)
    from_seats(row_all, all_s, all_r)
    gather.arrive()
    sa[...] = mm1(0, 0)
    for q in range(SEATS):
        for b in range(NK // 128):
            row_lanes[:, (q * 8 + b) * 128 : (q * 8 + b + 1) * 128] = row_all[q, b : b + 1, :]

    def step(i, carry):
        block, t = lax.div(i, STEPS), 2 * lax.rem(i, STEPS)
        nxt, prv = lax.rem(i + 1, 2 * STEPS), lax.rem(i + 2 * STEPS - 1, 2 * STEPS)
        before = mm2(wb, 2 * lax.rem(prv, STEPS) + 1)
        sb[...] = mm1(block, t + 1)
        weigh(sa, wa, block, t)
        acc[lax.div(prv, STEPS)] += before
        now = mm2(wa, t)
        sa[...] = mm1(lax.div(nxt, STEPS), 2 * lax.rem(nxt, STEPS))
        weigh(sb, wb, block, t + 1)
        acc[block] += now
        pl.when(i == STEPS)(hand_over)
        return carry

    lax.fori_loop(0, 2 * STEPS, step, 0)
    acc[1] += mm2(wb, SEATS * NK // KT - 1)
    sums(1)
    swap_sums(0).wait()
    for ch in range(NCH):
        begin(ch)
    swap_sums(1).wait()
    update(0, 1)
    update(1, 0)
    to_seats(pots2, pot2_s, pot2_r)
    outs[0].stage2()
    outs[1].stage2()
    outs[0].stage3()
    outs[2].stage2()
    outs[1].stage3()
    outs[0].stage4()
    outs[2].stage3()
    outs[1].stage4()
    outs[2].stage4()
    from_seats(pots2, pot2_s, pot2_r)
    for q in range(SEATS):
        listpot_ref[q * BLOCKS : (q + 1) * BLOCKS, :] = pots2[q, 0:BLOCKS, :] * LN2
    for ch in range(NCH):
        keep(ch).wait()
        outs[ch].arrive()
        outs[ch].sent()
    gather.sent()
    for copy in sent:
        copy.wait_send()


def local(key_rows, centroids):
    vmem = pl.BlockSpec(memory_space=pltpu.VMEM)
    dma = pltpu.SemaphoreType.DMA
    small = (8, 128)
    new, row_pot, list_pot = pl.pallas_call(
        kernel,
        out_shape=(
            pltpu.VMEM((NL, D), bf16),
            jax.ShapeDtypeStruct(small, f32),
            jax.ShapeDtypeStruct((NL // 128, 128), f32),
        ),
        in_specs=[pl.BlockSpec(memory_space=pltpu.HBM)] * 2,
        out_specs=(pl.BlockSpec(memory_space=pl.ANY), vmem, vmem),
        scratch_shapes=[
            pltpu.VMEM((NK, D), bf16),
            pltpu.VMEM((NL, D), bf16),
            dma((2,)),
            pltpu.VMEM((NT // 2, 2, 2, HALF, W), f32),
            pltpu.VMEM((NK, 128), f32),
            pltpu.VMEM((NK, 128), f32),
            pltpu.VMEM((NK, 128), f32),
            pltpu.VMEM(small, f32),
            pltpu.VMEM((2, NT, 8, W), f32),
            pltpu.VMEM((2, SEATS, 2, *small), f32),
            pltpu.VMEM((SEATS, *small), f32),
            pltpu.VMEM((SEATS, *small), f32),
            pltpu.VMEM((SEATS, *small), f32),
            pltpu.VMEM((2, N_LIST, *small), f32),
            pltpu.VMEM((N_LIST, *small), f32),
            pltpu.VMEM((N_ROW, *small), f32),
            pltpu.VMEM((SEATS, *small), f32),
            pltpu.VMEM((SEATS, NK, D), bf16),
            pltpu.VMEM((1, SEATS * NK), f32),
            pltpu.VMEM((SHARE, 128), f32),
            pltpu.VMEM((LB, KT), f32),
            pltpu.VMEM((LB, KT), f32),
            pltpu.VMEM((LB, KT), bf16),
            pltpu.VMEM((LB, KT), bf16),
            pltpu.VMEM((2, LB, D), f32),
            pltpu.VMEM((NCH, PIECE, D), bf16),
            pltpu.VMEM((NCH, PIECE, D), bf16),
            pltpu.VMEM((NCH, PIECE, D), bf16),
            pltpu.VMEM((2, LB, 128), f32),
            pltpu.VMEM((2, *small), f32),
            pltpu.VMEM((2, *small), f32),
            dma((2, N_LIST)), dma((2, N_LIST)), dma((N_LIST,)), dma((N_LIST,)),
            dma((N_ROW,)), dma((N_ROW,)), dma((2,)), dma((2,)),
            dma((SEATS,)), dma((SEATS,)), dma((SEATS,)), dma((SEATS,)), dma((SEATS,)), dma((SEATS,)),
            dma((20,)), dma((20,)), dma((NCH,)), dma((NCH,)), dma((NCH, 20)), dma((NCH, 20)), dma((NCH,)),
        ],
        compiler_params=pltpu.CompilerParams(
            collective_id=0, has_side_effects=True, vmem_limit_bytes=VMEM
        ),
        name="sinkhorn",
    )(key_rows, centroids)
    return new, row_pot.reshape(NK), list_pot.reshape(NL)


def solution(mesh):
    return jax.shard_map(
        local,
        mesh=mesh,
        in_specs=(P("row", None), P("list", None)),
        out_specs=(P("list", None), P("row"), P("list")),
        check_vma=False,
    )
```

```python
import math

import jax
import jax.numpy as jnp
from jax import lax
from jax.experimental import pallas as pl
from jax.experimental.pallas import tpu as pltpu
from jax.sharding import PartitionSpec as P

MESH = pl.DeviceIdType.MESH
f32 = jnp.float32
bf16 = jnp.bfloat16
LOG2E = math.log2(math.e)
LN2 = math.log(2.0)

D = 256
SCALE = 2.0 / math.sqrt(D) * LOG2E
NK = 1024
NL = 6144
W = 512
NT = NL // W
HALF = NK // 2
N_ROW, N_LIST, SEATS = 16, 8, 8
FAR_FIRST = (*range(6, 11), 5, 11, 4, 12, 13, 3, 14, 2, 15, 1)
SHARE = NL // SEATS
BLOCKS = SHARE // 128
LB = SHARE // 2
PIECE = 128
NCH = LB // PIECE
VMEM = 243 * 2**18
LOG2_KEYS = math.log2(NK * N_ROW)
LOG2_LISTS = math.log2(NL * N_LIST)
NT_DIMS = (((1,), (1,)), ((), ()))
NN_DIMS = (((1,), (0,)), ((), ()))


def tree(op, xs):
    xs = list(xs)
    while len(xs) > 1:
        ys = [op(a, b) for a, b in zip(xs[::2], xs[1::2])]
        if len(xs) % 2:
            ys.append(xs[-1])
        xs = ys
    return xs[0]


def log2(x):
    return jnp.log(x) * LOG2E


def fold(op, x):
    return tree(op, [x[8 * i : 8 * i + 8] for i in range(x.shape[0] // 8)])


def score_tile(keys, cents, scores, peak, i, half, part):
    rb = 32
    lists = pl.ds(pl.multiple_of((2 * i + half) * W, W), W)
    mine = keys[part * HALF : (part + 1) * HALF, :]
    s = lax.dot_general(mine, cents[lists, :], NT_DIMS, preferred_element_type=f32) * SCALE
    scores[i, half, part] = s
    for b in range(HALF // rb):
        rows = slice(part * HALF + b * rb, part * HALF + (b + 1) * rb)
        xs = [s[b * rb : (b + 1) * rb, v * 128 : (v + 1) * 128] for v in range(W // 128)]
        peak[rows, :] = jnp.maximum(peak[rows, :], tree(jnp.maximum, xs))


def sum_tile(scores, peak, total, i, half, part):
    rb = 32
    for b in range(HALF // rb):
        rows = slice(part * HALF + b * rb, part * HALF + (b + 1) * rb)
        top = peak[rows, :]
        xs = [scores[i, half, part, b * rb : (b + 1) * rb, v * 128 : (v + 1) * 128] for v in range(W // 128)]
        total[rows, :] += tree(jnp.add, [jnp.exp2(x - top) for x in xs])


def row_pass(work):
    def body(i, carry):
        for half in range(2):
            for step in work:
                step(i, half)
        return carry

    lax.fori_loop(0, NT // 2, body, 0)


def column_pass(scores, row_pot, stats, part, first, last):
    rb = 64
    columns = [(half, v) for half in range(2) for v in range(W // 128)]

    def body(i, carry):
        def at(n, b):
            half, v = columns[n]
            return i, half, part, slice(b * rb, (b + 1) * rb), slice(v * 128, (v + 1) * 128)

        top = None
        for n in range(len(columns) + 1):
            peaks = sums = None
            for b in range(HALF // rb):
                if n < len(columns):
                    x = scores[at(n, b)] + row_pot[part * HALF + b * rb : part * HALF + (b + 1) * rb, :]
                    scores[at(n, b)] = x
                    x = fold(jnp.maximum, x)
                    peaks = x if b == 0 else jnp.maximum(peaks, x)
                if n > 0:
                    e = jnp.exp2(scores[at(n - 1, b)] - top)
                    scores[at(n - 1, b)] = e
                    e = fold(jnp.add, e)
                    sums = e if b == 0 else sums + e
            if n > 0:
                j = i * len(columns) + n - 1
                q, row = lax.div(j, BLOCKS), lax.rem(j, BLOCKS)
                stats[part, pl.ds(q, 1), 0, pl.ds(row, 1), :] = top[None]
                stats[part, pl.ds(q, 1), 1, pl.ds(row, 1), :] = jnp.sum(sums, axis=0, keepdims=True)[None]
            if n < len(columns):
                top = jnp.max(peaks, axis=0, keepdims=True)
        return carry

    lax.fori_loop(first, last, body, 0)


def row_sums(scores, gain, total, part):
    rb, group = 64, 4

    def body(i, carry):
        def at(b):
            return pl.ds(pl.multiple_of(i * rb + 8 * b, 8), 8)

        def out(b):
            return pl.ds(pl.multiple_of(part * HALF + i * rb + 8 * b, 8), 8)

        def inner(c, accs):
            accs = list(accs)
            for t in range(group):
                for v in range(W // 128):
                    lanes = slice(v * 128, (v + 1) * 128)
                    g = gain[part, c * group + t, :, lanes]
                    for b in range(rb // 8):
                        accs[b] = accs[b] + scores[c * (group // 2) + t // 2, t % 2, part, at(b), lanes] * g
            return tuple(accs)

        zero = jnp.zeros((8, 128), f32)
        accs = lax.fori_loop(0, NT // group, inner, (zero,) * (rb // 8))
        for b in range(rb // 8):
            total[out(b), :] = accs[b]
        return carry

    lax.fori_loop(0, HALF // rb, body, 0)


def spread(compact, n, out, first=0):
    for b in range(n):
        out[first + b * 128 : first + (b + 1) * 128, :] = jnp.broadcast_to(compact[b : b + 1, :], (128, 128)).T


def remote(src, dst, send, recv, target):
    return pltpu.make_async_remote_copy(
        src_ref=src, dst_ref=dst, send_sem=send, recv_sem=recv, device_id=target, device_id_type=MESH
    )


class Gather:
    def __init__(self, at, send, recv, y, x, core, own, ring=False):
        self.at, self.send, self.recv = at, send, recv
        self.y, self.x, self.core, self.own, self.ring = y, x, core, own, ring

        def device(dy, flip, of=core):
            return {"row": (lax.rem(y + dy + 4, 4) * 2 + (1 - x if flip else x)) * 2 + of}

        up, down, side = device(1, False), device(-1, False), device(0, True)
        self.other = device(0, False, 1 - core)
        self.moves = [
            (up, (0, False), (-1, False), None),
            (down, (0, False), (1, False), None),
            (up, (-1, False), (-2, False), 0),
            (down, (1, False), (2, False), 1),
            (side, (0, False), (0, True), None),
            (up, (0, True), (-1, True), None),
            (down, (0, True), (1, True), None),
            (side, (-2, False), (2, True), 0),
            (side, (2, False), (2, True), 1),
        ]
        self.used = range(4) if ring else range(9)

    def place(self, block, part, *of):
        dy, flip = block
        return self.at(lax.rem(self.y + dy + 4, 4), 1 - self.x if flip else self.x, part, *of)

    def source(self, block, part):
        return self.own if block == (0, False) else self.place(block, part)

    def copy(self, m):
        target, sent, _, part = self.moves[m]
        return remote(self.source(sent, part), self.place(sent, part), self.send.at[m], self.recv.at[m], target)

    def arrival(self, m):
        target, _, came, part = self.moves[m]
        place = self.place(came, part)
        return remote(place, place, self.send.at[m], self.recv.at[m], target)

    def brought(self, m):
        return ((0, False), None) if m == 9 else self.moves[m][2:]

    def hand(self, m):
        block, part = self.brought(m)
        return remote(
            self.source(block, part), self.place(block, part), self.send.at[10 + m], self.recv.at[10 + m], self.other
        )

    def handed(self, m):
        block, part = self.brought(m)
        place = self.place(block, part, 1 - self.core)
        return remote(place, place, self.send.at[10 + m], self.recv.at[10 + m], self.other)

    def take(self, m, *sends):
        if m in self.used:
            self.arrival(m).wait_recv()
            for n in sends:
                if n in self.used:
                    self.copy(n).start()
            self.hand(m).start()

    def stage1(self):
        for m in (0, 1, 4):
            if m in self.used:
                self.copy(m).start()
        self.hand(9).start()

    def stage2(self):
        self.take(0, 2)
        self.take(1, 3)
        self.take(4, 5, 6)

    def stage3(self):
        self.take(2, 7)
        self.take(3, 8)

    def stage4(self):
        for m in (5, 6, 7, 8):
            self.take(m)

    def arrive(self, moves=range(10)):
        for m in moves:
            if m not in (*self.used, 9):
                continue
            self.handed(m).wait_recv()

    def sent(self):
        for m in self.used:
            self.copy(m).wait_send()
        for m in (*self.used, 9):
            self.hand(m).wait_send()


def kernel(
    keys_hbm, cents_hbm, new_ref, rowpot_ref, listpot_ref,
    keys, cents, load, scores, peak, total, row_pot, row1, gain, stats, both, pots, pots2, from_list1, from_list3, from_row2,
    row_all, keys_all, row_lanes, list_lanes, late, wa, wb, acc, give, came, done, tsum, tmine, tcame,
    list1_s, list1_r, list3_s, list3_r, row2_s, row2_r, tsum_s, tsum_r, pot_s, pot_r, pot2_s, pot2_r, all_s, all_r,
    keys_s, keys_r, twin_s, twin_r, out_s, out_r, here,
):
    row, lst = lax.axis_index("row"), lax.axis_index("list")
    core, x, y = lax.rem(row, 2), lax.rem(lax.div(row, 2), 2), lax.div(row, 4)
    seat = y * 2 + core

    def device(at, x):
        return (lax.div(at, 2) * 2 + x) * 2 + lax.rem(at, 2)

    def seat_of(device):
        return lax.div(device, 4) * 2 + lax.rem(device, 2)

    barrier = pltpu.get_barrier_semaphore()
    for k in range(1, N_ROW):
        pl.semaphore_signal(barrier, inc=1, device_id={"row": lax.rem(row + k, N_ROW)}, device_id_type=MESH)
    for k in range(1, N_LIST):
        pl.semaphore_signal(barrier, inc=1, device_id={"list": lax.rem(lst + k, N_LIST)}, device_id_type=MESH)
    stats[...] = jnp.ones(stats.shape, f32)
    tmine[...] = jnp.zeros(tmine.shape, f32)
    pots2[...] = jnp.zeros(pots2.shape, f32)
    peak[...] = jnp.full(peak.shape, -1e30, f32)
    total[...] = jnp.zeros(total.shape, f32)
    loads = [
        pltpu.make_async_copy(keys_hbm, keys, load.at[0]),
        pltpu.make_async_copy(cents_hbm, cents, load.at[1]),
    ]
    for copy in loads:
        copy.start()

    def score(part):
        return lambda i, half: score_tile(keys, cents, scores, peak, i, half, part)

    def add(part):
        return lambda i, half: sum_tile(scores, peak, total, i, half, part)

    n = HALF // 128

    def prepare(part):
        for b in range(n):
            rows = slice(part * HALF + b * 128, part * HALF + (b + 1) * 128)
            top = peak[rows, :].T
            best = jnp.max(top, axis=0, keepdims=True)
            from_list1[part, lst, b : b + 1, :] = best
            from_list1[part, lst, n + b : n + b + 1, :] = jnp.sum(
                total[rows, :].T * jnp.exp2(top - best), axis=0, keepdims=True
            )

    for copy in loads:
        copy.wait()
    keys_all[seat] = keys[...]
    row_pass([score(0)])
    row_pass([score(1), add(0)])
    prepare(0)
    pl.semaphore_wait(barrier, N_ROW + N_LIST - 2)

    def keys_at(y, x, part, of=core):
        at = y * 2 + of
        return keys_all.at[at] if part is None else keys_all.at[at, pl.ds(part * (NK // 2), NK // 2)]

    gather = Gather(keys_at, keys_s, keys_r, y, x, core, keys, ring=True)
    gather.stage1()
    sent = []

    def start(copies):
        for copy in copies:
            copy.start()
            sent.append(copy)

    def to_list(buf, send, recv):
        start(
            remote(buf.at[lst], buf.at[lst], send.at[k], recv.at[lst], {"list": lax.rem(lst + k, N_LIST)})
            for k in (5, 3, 7, 1, 4, 6, 2)
        )

    def from_list(buf, send, recv):
        for k in range(1, N_LIST):
            src = lax.rem(lst + k, N_LIST)
            remote(buf.at[src], buf.at[src], send.at[k], recv.at[src], {"list": src}).wait_recv()

    def to_row(src_of, buf, send, recv):
        to = [lax.rem(row + k, N_ROW) for k in FAR_FIRST]
        start(
            remote(src_of.at[seat_of(t)], buf.at[row], send.at[k + 1], recv.at[row], {"row": t})
            for k, t in enumerate(to)
        )

    def from_row(buf, send, recv):
        for k in range(1, N_ROW):
            src = lax.rem(row + k, N_ROW)
            remote(buf.at[src], buf.at[src], send.at[k], recv.at[src], {"row": src}).wait_recv()

    def to_seats(buf, send, recv):
        to = [lax.rem(seat + k, SEATS) for k in (4, 5, 3, 6, 2, 7, 1)]
        start(
            remote(buf.at[seat], buf.at[seat], send.at[k + 1], recv.at[seat], {"row": device(t, x)})
            for k, t in enumerate(to)
        )

    def from_seats(buf, send, recv):
        for k in range(1, SEATS):
            src = lax.rem(seat + k, SEATS)
            remote(buf.at[src], buf.at[src], send.at[k], recv.at[src], {"row": device(src, x)}).wait_recv()

    def tell(part):
        to_list(from_list1.at[part], list1_s.at[part], list1_r.at[part])

    def learn(part):
        from_list(from_list1.at[part], list1_s.at[part], list1_r.at[part])
        best = tree(jnp.maximum, [from_list1[part, k, 0:n] for k in range(N_LIST)])
        whole = tree(
            jnp.add, [from_list1[part, k, n : 2 * n] * jnp.exp2(from_list1[part, k, 0:n] - best) for k in range(N_LIST)]
        )
        row1[part * n : (part + 1) * n, :] = -LOG2_KEYS - (best + log2(whole))
        spread(row1[part * n : (part + 1) * n, :], n, row_pot, part * HALF)

    tell(0)
    row_pass([add(1)])
    prepare(1)
    tell(1)

    learn(0)
    column_pass(scores, row_pot, stats, 0, 0, NT // 2)
    learn(1)
    column_pass(scores, row_pot, stats, 1, 0, NT // 2)
    for q in range(SEATS):
        best = jnp.maximum(stats[0, q, 0], stats[1, q, 0])
        both[q] = best + log2(tree(jnp.add, [stats[p, q, 1] * jnp.exp2(stats[p, q, 0] - best) for p in range(2)]))
    from_row2[row] = both[seat]
    to_row(both, from_row2, row2_s, row2_r)
    from_row(from_row2, row2_s, row2_r)
    best = tree(jnp.maximum, [from_row2[k] for k in range(N_ROW)])
    whole = tree(jnp.add, [jnp.exp2(from_row2[k] - best) for k in range(N_ROW)])
    pots[seat] = -LOG2_LISTS - (best + log2(whole))
    to_seats(pots, pot_s, pot_r)
    from_seats(pots, pot_s, pot_r)
    gather.stage2()

    for q in range(SEATS):
        for p in range(2):
            g = jnp.exp2(stats[p, q, 0] + pots[q])
            for b in range(BLOCKS):
                j = q * BLOCKS + b
                v = j % (W // 128)
                gain[p, j // (W // 128), :, v * 128 : (v + 1) * 128] = jnp.broadcast_to(g[b : b + 1, :], (8, 128))
    row_sums(scores, gain, total, 0)
    row_sums(scores, gain, total, 1)
    for b in range(NK // 128):
        from_list3[lst, b : b + 1, :] = jnp.sum(total[b * 128 : (b + 1) * 128, :].T, axis=0, keepdims=True)
    to_list(from_list3, list3_s, list3_r)

    firsts = ((1 - x) * LB, x * LB)

    def seat_at(k):
        j = lax.div(k, 2)
        far = j + lax.div(j, 2) - 2 * lax.div(j, 3)
        return lax.rem(y + far, 4) * 2 + lax.rem(k, 2)

    def late_scores(k, carry):
        tile = keys_all[seat_at(k)]
        for side_ in range(2):
            lists = pl.ds(pl.multiple_of(seat * SHARE + firsts[side_], 128), LB)
            for h in range(2):
                s = lax.dot_general(cents[lists, :], tile[h * W : (h + 1) * W], NT_DIMS, preferred_element_type=f32)
                if side_ == 0:
                    late[k, h] = s
                else:
                    scores[lax.div(k, 2), lax.rem(k, 2), h, 0:LB, :] = s
        return carry

    gather.arrive((0, 1, 9))
    lax.fori_loop(0, 6, late_scores, 0)
    from_list(from_list3, list3_s, list3_r)
    delta = -LOG2_KEYS - log2(tree(jnp.add, [from_list3[k] for k in range(N_LIST)]))
    row2 = row1[...] + delta
    row_all[seat] = row2
    to_seats(row_all, all_s, all_r)
    rowpot_ref[...] = row2 * LN2
    spread(pots[seat] + LOG2_LISTS, BLOCKS, list_lanes)
    acc[...] = jnp.zeros(acc.shape, f32)
    tsum[...] = jnp.zeros(tsum.shape, f32)
    gather.stage3()
    gather.arrive((2, 3))
    lax.fori_loop(6, SEATS, late_scores, 0)

    def piece_at(ch):
        def at(y, x, part, of=core):
            first = pl.multiple_of((y * 2 + of) * SHARE + x * LB + ch * PIECE, PIECE)
            if part is None:
                return new_ref.at[pl.ds(first, PIECE)]
            return new_ref.at[pl.ds(pl.multiple_of(first + part * (PIECE // 2), PIECE // 2), PIECE // 2)]

        return at

    outs = [Gather(piece_at(ch), out_s.at[ch], out_r.at[ch], y, x, core, done.at[ch]) for ch in range(NCH)]
    side = {"row": device(seat, 1 - x)}

    def swap(ch):
        return remote(give.at[ch], came.at[ch], twin_s.at[ch], twin_r.at[ch], side)

    def swap_sums(block):
        return remote(tmine.at[block], tcame.at[block], tsum_s.at[block], tsum_r.at[block], side)

    def sums(side_, pieces):
        for b in pieces:
            rows = slice(b * 128, (b + 1) * 128)
            tmine[side_, b : b + 1, :] = jnp.sum(tsum[side_, rows, :].T, axis=0, keepdims=True)

    def hand_over():
        sums(0, range(NCH))
        swap_sums(0).start()
        for ch in range(NCH):
            give[ch] = acc[0, ch * PIECE : (ch + 1) * PIECE, :].astype(bf16)
            swap(ch).start()

    def keep(ch):
        return pltpu.make_async_copy(done.at[ch], piece_at(ch)(y, x, None), here.at[ch])

    def begin(ch):
        whole = tmine[1, ch : ch + 1, :] + tcame[0, ch : ch + 1, :]
        scale = jnp.broadcast_to(1.0 / whole, (PIECE, 128)).T
        swap(ch).wait()
        for v in range(D // 128):
            lanes = slice(v * 128, (v + 1) * 128)
            summed = acc[1, ch * PIECE : (ch + 1) * PIECE, lanes] + came[ch, :, lanes].astype(f32)
            done[ch, :, lanes] = (summed * scale).astype(bf16)
        outs[ch].stage1()
        keep(ch).start()

    def update(block, other):
        for b in range(NCH):
            at = pl.ds((x if block else 1 - x) * NCH + b, 1)
            whole = tmine[block, b : b + 1, :] + tcame[other, b : b + 1, :]
            pots2[seat, at, :] = pots[seat, at, :] - log2(whole)

    def run(side_):
        lists = pl.ds(pl.multiple_of(firsts[side_], 128), LB)

        def sum_up(w_ref, k):
            return lax.dot_general(w_ref[...], keys_all[seat_at(k)], NN_DIMS, preferred_element_type=f32)

        def weigh(w_ref, k, odd):
            c = list_lanes[lists, :]
            parts = []
            for v in range(NK // 128):
                h, u = v // (W // 128), v % (W // 128)
                lanes = slice(u * 128, (u + 1) * 128)
                s = late[k, h, :, lanes] if side_ == 0 else scores[lax.div(k, 2), odd, h, 0:LB, lanes]
                r = row_lanes[k, :, v * 128 : (v + 1) * 128]
                w = jnp.exp2((s * SCALE + r) + c)
                w_ref[:, v * 128 : (v + 1) * 128] = w.astype(bf16)
                parts.append(w)
            tsum[side_] += tree(jnp.add, parts)

        def step(i, carry):
            before = sum_up(wb, lax.rem(2 * i + SEATS - 1, SEATS))
            weigh(wa, 2 * i, 0)
            acc[side_] += before
            now = sum_up(wa, 2 * i)
            weigh(wb, 2 * i + 1, 1)
            acc[side_] += now
            return carry

        wb[...] = jnp.zeros(wb.shape, bf16)
        lax.fori_loop(0, SEATS // 2, step, 0)
        acc[side_] += sum_up(wb, SEATS - 1)

    from_seats(row_all, all_s, all_r)
    for k in range(SEATS):
        for b in range(NK // 128):
            row_lanes[k, :, b * 128 : (b + 1) * 128] = row_all[seat_at(k), b : b + 1, :]
    run(0)
    hand_over()
    run(1)
    sums(1, range(NCH))
    swap_sums(0).wait()
    begin(0)
    swap_sums(1).start()
    for ch in range(1, NCH):
        begin(ch)
    outs[0].stage2()
    swap_sums(1).wait()
    update(0, 1)
    update(1, 0)
    to_seats(pots2, pot2_s, pot2_r)
    outs[1].stage2()
    outs[0].stage3()
    outs[2].stage2()
    outs[1].stage3()
    outs[0].stage4()
    outs[2].stage3()
    outs[1].stage4()
    outs[2].stage4()
    from_seats(pots2, pot2_s, pot2_r)
    for q in range(SEATS):
        listpot_ref[q * BLOCKS : (q + 1) * BLOCKS, :] = pots2[q, 0:BLOCKS, :] * LN2
    for ch in range(NCH):
        keep(ch).wait()
        outs[ch].arrive()
        outs[ch].sent()
    gather.sent()
    for copy in sent:
        copy.wait_send()


def local(key_rows, centroids):
    vmem = pl.BlockSpec(memory_space=pltpu.VMEM)
    dma = pltpu.SemaphoreType.DMA
    small = (8, 128)
    new, row_pot, list_pot = pl.pallas_call(
        kernel,
        out_shape=(
            pltpu.VMEM((NL, D), bf16),
            jax.ShapeDtypeStruct(small, f32),
            jax.ShapeDtypeStruct((NL // 128, 128), f32),
        ),
        in_specs=[pl.BlockSpec(memory_space=pltpu.HBM)] * 2,
        out_specs=(pl.BlockSpec(memory_space=pl.ANY), vmem, vmem),
        scratch_shapes=[
            pltpu.VMEM((NK, D), bf16),
            pltpu.VMEM((NL, D), bf16),
            dma((2,)),
            pltpu.VMEM((NT // 2, 2, 2, HALF, W), f32),
            pltpu.VMEM((NK, 128), f32),
            pltpu.VMEM((NK, 128), f32),
            pltpu.VMEM((NK, 128), f32),
            pltpu.VMEM(small, f32),
            pltpu.VMEM((2, NT, 8, W), f32),
            pltpu.VMEM((2, SEATS, 2, *small), f32),
            pltpu.VMEM((SEATS, *small), f32),
            pltpu.VMEM((SEATS, *small), f32),
            pltpu.VMEM((SEATS, *small), f32),
            pltpu.VMEM((2, N_LIST, *small), f32),
            pltpu.VMEM((N_LIST, *small), f32),
            pltpu.VMEM((N_ROW, *small), f32),
            pltpu.VMEM((SEATS, *small), f32),
            pltpu.VMEM((SEATS, NK, D), bf16),
            pltpu.VMEM((SEATS, 1, NK), f32),
            pltpu.VMEM((SHARE, 128), f32),
            pltpu.VMEM((SEATS, 2, LB, W), f32),
            pltpu.VMEM((LB, NK), bf16),
            pltpu.VMEM((LB, NK), bf16),
            pltpu.VMEM((2, LB, D), f32),
            pltpu.VMEM((NCH, PIECE, D), bf16),
            pltpu.VMEM((NCH, PIECE, D), bf16),
            pltpu.VMEM((NCH, PIECE, D), bf16),
            pltpu.VMEM((2, LB, 128), f32),
            pltpu.VMEM((2, *small), f32),
            pltpu.VMEM((2, *small), f32),
            dma((2, N_LIST)), dma((2, N_LIST)), dma((N_LIST,)), dma((N_LIST,)),
            dma((N_ROW,)), dma((N_ROW,)), dma((2,)), dma((2,)),
            dma((SEATS,)), dma((SEATS,)), dma((SEATS,)), dma((SEATS,)), dma((SEATS,)), dma((SEATS,)),
            dma((20,)), dma((20,)), dma((NCH,)), dma((NCH,)), dma((NCH, 20)), dma((NCH, 20)), dma((NCH,)),
        ],
        compiler_params=pltpu.CompilerParams(
            collective_id=0, has_side_effects=True, vmem_limit_bytes=VMEM
        ),
        name="sinkhorn",
    )(key_rows, centroids)
    return new, row_pot.reshape(NK), list_pot.reshape(NL)


def solution(mesh):
    return jax.shard_map(
        local,
        mesh=mesh,
        in_specs=(P("row", None), P("list", None)),
        out_specs=(P("list", None), P("row"), P("list")),
        check_vma=False,
    )
```

```python
import math

import jax
import jax.numpy as jnp
from jax import lax
from jax.experimental import pallas as pl
from jax.experimental.pallas import tpu as pltpu
from jax.sharding import PartitionSpec as P

MESH = pl.DeviceIdType.MESH
f32 = jnp.float32
bf16 = jnp.bfloat16
LOG2E = math.log2(math.e)
LN2 = math.log(2.0)

D = 256
SCALE = 2.0 / math.sqrt(D) * LOG2E
NK = 1024
NL = 6144
W = 512
NT = NL // W
HALF = NK // 2
N_ROW, N_LIST, SEATS = 16, 8, 8
FAR_FIRST = (*range(6, 11), 5, 11, 4, 12, 13, 3, 14, 2, 15, 1)
SHARE = NL // SEATS
BLOCKS = SHARE // 128
LB = SHARE // 2
PIECE = 128
NCH = LB // PIECE
VMEM = 243 * 2**18
LOG2_KEYS = math.log2(NK * N_ROW)
LOG2_LISTS = math.log2(NL * N_LIST)
NT_DIMS = (((1,), (1,)), ((), ()))
NN_DIMS = (((1,), (0,)), ((), ()))


def tree(op, xs):
    xs = list(xs)
    while len(xs) > 1:
        ys = [op(a, b) for a, b in zip(xs[::2], xs[1::2])]
        if len(xs) % 2:
            ys.append(xs[-1])
        xs = ys
    return xs[0]


def log2(x):
    return jnp.log(x) * LOG2E


def fold(op, x):
    return tree(op, [x[8 * i : 8 * i + 8] for i in range(x.shape[0] // 8)])


def score_tile(keys, cents, scores, peak, i, half, part):
    rb = 32
    lists = pl.ds(pl.multiple_of((2 * i + half) * W, W), W)
    mine = keys[part * HALF : (part + 1) * HALF, :]
    s = lax.dot_general(mine, cents[lists, :], NT_DIMS, preferred_element_type=f32) * SCALE
    scores[i, half, part] = s
    for b in range(HALF // rb):
        rows = slice(part * HALF + b * rb, part * HALF + (b + 1) * rb)
        xs = [s[b * rb : (b + 1) * rb, v * 128 : (v + 1) * 128] for v in range(W // 128)]
        peak[rows, :] = jnp.maximum(peak[rows, :], tree(jnp.maximum, xs))


def sum_tile(scores, peak, total, i, half, part):
    rb = 32
    for b in range(HALF // rb):
        rows = slice(part * HALF + b * rb, part * HALF + (b + 1) * rb)
        top = peak[rows, :]
        xs = [scores[i, half, part, b * rb : (b + 1) * rb, v * 128 : (v + 1) * 128] for v in range(W // 128)]
        total[rows, :] += tree(jnp.add, [jnp.exp2(x - top) for x in xs])


def row_pass(work):
    def body(i, carry):
        for half in range(2):
            for step in work:
                step(i, half)
        return carry

    lax.fori_loop(0, NT // 2, body, 0)


def column_pass(scores, row_pot, stats, part, first, last):
    rb = 64
    columns = [(half, v) for half in range(2) for v in range(W // 128)]

    def body(i, carry):
        def at(n, b):
            half, v = columns[n]
            return i, half, part, slice(b * rb, (b + 1) * rb), slice(v * 128, (v + 1) * 128)

        top = None
        for n in range(len(columns) + 1):
            peaks = sums = None
            for b in range(HALF // rb):
                if n < len(columns):
                    x = scores[at(n, b)] + row_pot[part * HALF + b * rb : part * HALF + (b + 1) * rb, :]
                    scores[at(n, b)] = x
                    x = fold(jnp.maximum, x)
                    peaks = x if b == 0 else jnp.maximum(peaks, x)
                if n > 0:
                    e = jnp.exp2(scores[at(n - 1, b)] - top)
                    scores[at(n - 1, b)] = e
                    e = fold(jnp.add, e)
                    sums = e if b == 0 else sums + e
            if n > 0:
                j = i * len(columns) + n - 1
                q, row = lax.div(j, BLOCKS), lax.rem(j, BLOCKS)
                stats[part, pl.ds(q, 1), 0, pl.ds(row, 1), :] = top[None]
                stats[part, pl.ds(q, 1), 1, pl.ds(row, 1), :] = jnp.sum(sums, axis=0, keepdims=True)[None]
            if n < len(columns):
                top = jnp.max(peaks, axis=0, keepdims=True)
        return carry

    lax.fori_loop(first, last, body, 0)


def row_sums(scores, gain, total, part):
    rb, group = 64, 4

    def body(i, carry):
        def at(b):
            return pl.ds(pl.multiple_of(i * rb + 8 * b, 8), 8)

        def out(b):
            return pl.ds(pl.multiple_of(part * HALF + i * rb + 8 * b, 8), 8)

        def inner(c, accs):
            accs = list(accs)
            for t in range(group):
                for v in range(W // 128):
                    lanes = slice(v * 128, (v + 1) * 128)
                    g = gain[part, c * group + t, :, lanes]
                    for b in range(rb // 8):
                        accs[b] = accs[b] + scores[c * (group // 2) + t // 2, t % 2, part, at(b), lanes] * g
            return tuple(accs)

        zero = jnp.zeros((8, 128), f32)
        accs = lax.fori_loop(0, NT // group, inner, (zero,) * (rb // 8))
        for b in range(rb // 8):
            total[out(b), :] = accs[b]
        return carry

    lax.fori_loop(0, HALF // rb, body, 0)


def spread(compact, n, out, first=0):
    for b in range(n):
        out[first + b * 128 : first + (b + 1) * 128, :] = jnp.broadcast_to(compact[b : b + 1, :], (128, 128)).T


def remote(src, dst, send, recv, target):
    return pltpu.make_async_remote_copy(
        src_ref=src, dst_ref=dst, send_sem=send, recv_sem=recv, device_id=target, device_id_type=MESH
    )


class Gather:
    def __init__(self, at, send, recv, y, x, core, own, ring=False, lean=0):
        self.at, self.send, self.recv = at, send, recv
        self.y, self.x, self.core, self.own, self.ring = y, x, core, own, ring

        def device(dy, flip, of=core):
            return {"row": (lax.rem(y + dy + 4, 4) * 2 + (1 - x if flip else x)) * 2 + of}

        up, down, side = device(1, False), device(-1, False), device(0, True)
        self.other = device(0, False, 1 - core)
        self.moves = [
            (up, (0, False), (-1, False), None),
            (down, (0, False), (1, False), None),
            (up, (-1, False), (-2, False), 0),
            (down, (1, False), (2, False), 1),
            (side, (0, False), (0, True), None),
            (up, (0, True), (-1, True), None),
            (down, (0, True), (1, True), None),
            (side, (-2, False), (2, True), 0),
            (side, (2, False), (2, True), 1),
        ]
        if lean:
            m = 5 if lean < 0 else 6
            block = (-1, False) if lean < 0 else (1, False)
            self.moves[m] = (side, block, (block[0], True), None)
        self.lean = lean
        self.used = range(4) if ring else range(9)

    def place(self, block, part, *of):
        dy, flip = block
        return self.at(lax.rem(self.y + dy + 4, 4), 1 - self.x if flip else self.x, part, *of)

    def source(self, block, part):
        return self.own if block == (0, False) else self.place(block, part)

    def copy(self, m):
        target, sent, _, part = self.moves[m]
        return remote(self.source(sent, part), self.place(sent, part), self.send.at[m], self.recv.at[m], target)

    def arrival(self, m):
        target, _, came, part = self.moves[m]
        place = self.place(came, part)
        return remote(place, place, self.send.at[m], self.recv.at[m], target)

    def brought(self, m):
        return ((0, False), None) if m == 9 else self.moves[m][2:]

    def hand(self, m):
        block, part = self.brought(m)
        return remote(
            self.source(block, part), self.place(block, part), self.send.at[10 + m], self.recv.at[10 + m], self.other
        )

    def handed(self, m):
        block, part = self.brought(m)
        place = self.place(block, part, 1 - self.core)
        return remote(place, place, self.send.at[10 + m], self.recv.at[10 + m], self.other)

    def take(self, m, *sends):
        if m in self.used:
            self.arrival(m).wait_recv()
            for n in sends:
                if n in self.used:
                    self.copy(n).start()
            self.hand(m).start()

    def stage1(self):
        for m in (0, 1, 4):
            if m in self.used:
                self.copy(m).start()
        self.hand(9).start()

    def stage2(self):
        self.take(0, 2, *((5,) if self.lean < 0 else ()))
        self.take(1, 3, *((6,) if self.lean > 0 else ()))
        self.take(4, *((5,) if self.lean >= 0 else ()), *((6,) if self.lean <= 0 else ()))

    def stage3(self):
        self.take(2, 7)
        self.take(3, 8)

    def stage4(self):
        for m in (5, 6, 7, 8):
            self.take(m)

    def arrive(self, moves=range(10)):
        for m in moves:
            if m not in (*self.used, 9):
                continue
            self.handed(m).wait_recv()

    def sent(self):
        for m in self.used:
            self.copy(m).wait_send()
        for m in (*self.used, 9):
            self.hand(m).wait_send()


def kernel(
    keys_hbm, cents_hbm, new_ref, rowpot_ref, listpot_ref,
    keys, cents, load, scores, peak, total, row_pot, row1, gain, stats, both, pots, pots2, from_list1, from_list3, from_row2,
    row_all, keys_all, row_lanes, list_lanes, late, wa, wb, acc, give, came, done, tsum, tmine, tcame,
    list1_s, list1_r, list3_s, list3_r, row2_s, row2_r, tsum_s, tsum_r, pot_s, pot_r, pot2_s, pot2_r, all_s, all_r,
    keys_s, keys_r, twin_s, twin_r, out_s, out_r, here,
):
    row, lst = lax.axis_index("row"), lax.axis_index("list")
    core, x, y = lax.rem(row, 2), lax.rem(lax.div(row, 2), 2), lax.div(row, 4)
    seat = y * 2 + core

    def device(at, x):
        return (lax.div(at, 2) * 2 + x) * 2 + lax.rem(at, 2)

    def seat_of(device):
        return lax.div(device, 4) * 2 + lax.rem(device, 2)

    barrier = pltpu.get_barrier_semaphore()
    for k in range(1, N_ROW):
        pl.semaphore_signal(barrier, inc=1, device_id={"row": lax.rem(row + k, N_ROW)}, device_id_type=MESH)
    for k in range(1, N_LIST):
        pl.semaphore_signal(barrier, inc=1, device_id={"list": lax.rem(lst + k, N_LIST)}, device_id_type=MESH)
    stats[...] = jnp.ones(stats.shape, f32)
    tmine[...] = jnp.zeros(tmine.shape, f32)
    pots2[...] = jnp.zeros(pots2.shape, f32)
    peak[...] = jnp.full(peak.shape, -1e30, f32)
    total[...] = jnp.zeros(total.shape, f32)
    loads = [
        pltpu.make_async_copy(keys_hbm, keys, load.at[0]),
        pltpu.make_async_copy(cents_hbm, cents, load.at[1]),
    ]
    for copy in loads:
        copy.start()

    def score(part):
        return lambda i, half: score_tile(keys, cents, scores, peak, i, half, part)

    def add(part):
        return lambda i, half: sum_tile(scores, peak, total, i, half, part)

    n = HALF // 128

    def prepare(part):
        for b in range(n):
            rows = slice(part * HALF + b * 128, part * HALF + (b + 1) * 128)
            top = peak[rows, :].T
            best = jnp.max(top, axis=0, keepdims=True)
            from_list1[part, lst, b : b + 1, :] = best
            from_list1[part, lst, n + b : n + b + 1, :] = jnp.sum(
                total[rows, :].T * jnp.exp2(top - best), axis=0, keepdims=True
            )

    for copy in loads:
        copy.wait()
    keys_all[seat] = keys[...]
    row_pass([score(0)])
    row_pass([score(1), add(0)])
    prepare(0)
    pl.semaphore_wait(barrier, N_ROW + N_LIST - 2)

    def keys_at(y, x, part, of=core):
        at = y * 2 + of
        return keys_all.at[at] if part is None else keys_all.at[at, pl.ds(part * (NK // 2), NK // 2)]

    gather = Gather(keys_at, keys_s, keys_r, y, x, core, keys, ring=True)
    gather.stage1()
    sent = []

    def start(copies):
        for copy in copies:
            copy.start()
            sent.append(copy)

    def to_list(buf, send, recv):
        start(
            remote(buf.at[lst], buf.at[lst], send.at[k], recv.at[lst], {"list": lax.rem(lst + k, N_LIST)})
            for k in (5, 3, 7, 1, 4, 6, 2)
        )

    def from_list(buf, send, recv):
        for k in range(1, N_LIST):
            src = lax.rem(lst + k, N_LIST)
            remote(buf.at[src], buf.at[src], send.at[k], recv.at[src], {"list": src}).wait_recv()

    def to_row(src_of, buf, send, recv):
        to = [lax.rem(row + k, N_ROW) for k in FAR_FIRST]
        start(
            remote(src_of.at[seat_of(t)], buf.at[row], send.at[k + 1], recv.at[row], {"row": t})
            for k, t in enumerate(to)
        )

    def from_row(buf, send, recv):
        for k in range(1, N_ROW):
            src = lax.rem(row + k, N_ROW)
            remote(buf.at[src], buf.at[src], send.at[k], recv.at[src], {"row": src}).wait_recv()

    def to_seats(buf, send, recv):
        to = [lax.rem(seat + k, SEATS) for k in (4, 5, 3, 6, 2, 7, 1)]
        start(
            remote(buf.at[seat], buf.at[seat], send.at[k + 1], recv.at[seat], {"row": device(t, x)})
            for k, t in enumerate(to)
        )

    def from_seats(buf, send, recv):
        for k in range(1, SEATS):
            src = lax.rem(seat + k, SEATS)
            remote(buf.at[src], buf.at[src], send.at[k], recv.at[src], {"row": device(src, x)}).wait_recv()

    def tell(part):
        to_list(from_list1.at[part], list1_s.at[part], list1_r.at[part])

    def learn(part):
        from_list(from_list1.at[part], list1_s.at[part], list1_r.at[part])
        best = tree(jnp.maximum, [from_list1[part, k, 0:n] for k in range(N_LIST)])
        whole = tree(
            jnp.add, [from_list1[part, k, n : 2 * n] * jnp.exp2(from_list1[part, k, 0:n] - best) for k in range(N_LIST)]
        )
        row1[part * n : (part + 1) * n, :] = -LOG2_KEYS - (best + log2(whole))
        spread(row1[part * n : (part + 1) * n, :], n, row_pot, part * HALF)

    tell(0)
    row_pass([add(1)])
    prepare(1)
    tell(1)

    learn(0)
    column_pass(scores, row_pot, stats, 0, 0, NT // 2)
    learn(1)
    column_pass(scores, row_pot, stats, 1, 0, NT // 2)
    for q in range(SEATS):
        best = jnp.maximum(stats[0, q, 0], stats[1, q, 0])
        both[q] = best + log2(tree(jnp.add, [stats[p, q, 1] * jnp.exp2(stats[p, q, 0] - best) for p in range(2)]))
    from_row2[row] = both[seat]
    to_row(both, from_row2, row2_s, row2_r)
    from_row(from_row2, row2_s, row2_r)
    best = tree(jnp.maximum, [from_row2[k] for k in range(N_ROW)])
    whole = tree(jnp.add, [jnp.exp2(from_row2[k] - best) for k in range(N_ROW)])
    pots[seat] = -LOG2_LISTS - (best + log2(whole))
    to_seats(pots, pot_s, pot_r)
    from_seats(pots, pot_s, pot_r)
    gather.stage2()

    for q in range(SEATS):
        for p in range(2):
            g = jnp.exp2(stats[p, q, 0] + pots[q])
            for b in range(BLOCKS):
                j = q * BLOCKS + b
                v = j % (W // 128)
                gain[p, j // (W // 128), :, v * 128 : (v + 1) * 128] = jnp.broadcast_to(g[b : b + 1, :], (8, 128))
    row_sums(scores, gain, total, 0)
    row_sums(scores, gain, total, 1)
    for b in range(NK // 128):
        from_list3[lst, b : b + 1, :] = jnp.sum(total[b * 128 : (b + 1) * 128, :].T, axis=0, keepdims=True)
    to_list(from_list3, list3_s, list3_r)

    firsts = ((1 - x) * LB, x * LB)

    def seat_at(k):
        j = lax.div(k, 2)
        far = j + lax.div(j, 2) - 2 * lax.div(j, 3)
        return lax.rem(y + far, 4) * 2 + lax.rem(k, 2)

    spread(pots[seat] + LOG2_LISTS, BLOCKS, list_lanes)

    def late_scores(k, carry):
        tile = keys_all[seat_at(k)]
        for side_ in range(2):
            lists = pl.ds(pl.multiple_of(seat * SHARE + firsts[side_], 128), LB)
            for h in range(2):
                s = lax.dot_general(cents[lists, :], tile[h * W : (h + 1) * W], NT_DIMS, preferred_element_type=f32)
                c = list_lanes[pl.ds(pl.multiple_of(firsts[side_], 128), LB), :]
                for v in range(W // 128):
                    lanes = slice(v * 128, (v + 1) * 128)
                    if side_ == 0:
                        late[k, h, :, lanes] = s[:, lanes] * SCALE + c
                    else:
                        scores[lax.div(k, 2), lax.rem(k, 2), h, 0:LB, lanes] = s[:, lanes] * SCALE + c
        return carry

    gather.arrive((0, 1, 9))
    lax.fori_loop(0, 6, late_scores, 0)
    from_list(from_list3, list3_s, list3_r)
    delta = -LOG2_KEYS - log2(tree(jnp.add, [from_list3[k] for k in range(N_LIST)]))
    row2 = row1[...] + delta
    row_all[seat] = row2
    to_seats(row_all, all_s, all_r)
    rowpot_ref[...] = row2 * LN2
    acc[...] = jnp.zeros(acc.shape, f32)
    tsum[...] = jnp.zeros(tsum.shape, f32)
    gather.stage3()
    gather.arrive((2, 3))
    lax.fori_loop(6, SEATS, late_scores, 0)

    def piece_at(ch):
        def at(y, x, part, of=core):
            first = pl.multiple_of((y * 2 + of) * SHARE + x * LB + ch * PIECE, PIECE)
            if part is None:
                return new_ref.at[pl.ds(first, PIECE)]
            return new_ref.at[pl.ds(pl.multiple_of(first + part * (PIECE // 2), PIECE // 2), PIECE // 2)]

        return at

    outs = [
        Gather(piece_at(ch), out_s.at[ch], out_r.at[ch], y, x, core, done.at[ch], lean=(1, -1, 0)[ch])
        for ch in range(NCH)
    ]
    side = {"row": device(seat, 1 - x)}

    def swap(ch):
        return remote(give.at[ch], came.at[ch], twin_s.at[ch], twin_r.at[ch], side)

    def swap_sums(block):
        return remote(tmine.at[block], tcame.at[block], tsum_s.at[block], tsum_r.at[block], side)

    def sums(side_, pieces):
        for b in pieces:
            rows = slice(b * 128, (b + 1) * 128)
            tmine[side_, b : b + 1, :] = jnp.sum(tsum[side_, rows, :].T, axis=0, keepdims=True)

    def hand_over():
        sums(0, range(NCH))
        swap_sums(0).start()
        for ch in range(NCH):
            give[ch] = acc[0, ch * PIECE : (ch + 1) * PIECE, :].astype(bf16)
            swap(ch).start()

    def keep(ch):
        return pltpu.make_async_copy(done.at[ch], piece_at(ch)(y, x, None), here.at[ch])

    def begin(ch):
        whole = tmine[1, ch : ch + 1, :] + tcame[0, ch : ch + 1, :]
        scale = jnp.broadcast_to(1.0 / whole, (PIECE, 128)).T
        swap(ch).wait()
        for v in range(D // 128):
            lanes = slice(v * 128, (v + 1) * 128)
            summed = acc[1, ch * PIECE : (ch + 1) * PIECE, lanes] + came[ch, :, lanes].astype(f32)
            done[ch, :, lanes] = (summed * scale).astype(bf16)
        outs[ch].stage1()
        keep(ch).start()

    def update(block, other):
        for b in range(NCH):
            at = pl.ds((x if block else 1 - x) * NCH + b, 1)
            whole = tmine[block, b : b + 1, :] + tcame[other, b : b + 1, :]
            pots2[seat, at, :] = pots[seat, at, :] - log2(whole)

    def run(side_):
        def sum_up(w_ref, k):
            return lax.dot_general(w_ref[...], keys_all[seat_at(k)], NN_DIMS, preferred_element_type=f32)

        def weigh(w_ref, k, odd):
            parts = []
            for v in range(NK // 128):
                h, u = v // (W // 128), v % (W // 128)
                lanes = slice(u * 128, (u + 1) * 128)
                s = late[k, h, :, lanes] if side_ == 0 else scores[lax.div(k, 2), odd, h, 0:LB, lanes]
                r = row_lanes[k, :, v * 128 : (v + 1) * 128]
                w = jnp.exp2(s + r)
                w_ref[:, v * 128 : (v + 1) * 128] = w.astype(bf16)
                parts.append(w)
            tsum[side_] += tree(jnp.add, parts)

        def step(i, carry):
            before = sum_up(wb, lax.rem(2 * i + SEATS - 1, SEATS))
            weigh(wa, 2 * i, 0)
            acc[side_] += before
            now = sum_up(wa, 2 * i)
            weigh(wb, 2 * i + 1, 1)
            acc[side_] += now
            return carry

        wb[...] = jnp.zeros(wb.shape, bf16)
        lax.fori_loop(0, SEATS // 2, step, 0)
        acc[side_] += sum_up(wb, SEATS - 1)

    from_seats(row_all, all_s, all_r)
    for k in range(SEATS):
        for b in range(NK // 128):
            row_lanes[k, :, b * 128 : (b + 1) * 128] = row_all[seat_at(k), b : b + 1, :]
    run(0)
    hand_over()
    run(1)
    sums(1, range(NCH))
    swap_sums(0).wait()
    for ch in range(NCH):
        begin(ch)
    swap_sums(1).start()
    for ch in range(NCH):
        outs[ch].stage2()
    outs[0].stage3()
    swap_sums(1).wait()
    update(0, 1)
    update(1, 0)
    to_seats(pots2, pot2_s, pot2_r)
    outs[1].stage3()
    outs[0].stage4()
    outs[2].stage3()
    outs[1].stage4()
    outs[2].stage4()
    from_seats(pots2, pot2_s, pot2_r)
    for q in range(SEATS):
        listpot_ref[q * BLOCKS : (q + 1) * BLOCKS, :] = pots2[q, 0:BLOCKS, :] * LN2
    for ch in range(NCH):
        keep(ch).wait()
        outs[ch].arrive()
        outs[ch].sent()
    gather.sent()
    for copy in sent:
        copy.wait_send()


def local(key_rows, centroids):
    vmem = pl.BlockSpec(memory_space=pltpu.VMEM)
    dma = pltpu.SemaphoreType.DMA
    small = (8, 128)
    new, row_pot, list_pot = pl.pallas_call(
        kernel,
        out_shape=(
            pltpu.VMEM((NL, D), bf16),
            jax.ShapeDtypeStruct(small, f32),
            jax.ShapeDtypeStruct((NL // 128, 128), f32),
        ),
        in_specs=[pl.BlockSpec(memory_space=pltpu.HBM)] * 2,
        out_specs=(pl.BlockSpec(memory_space=pl.ANY), vmem, vmem),
        scratch_shapes=[
            pltpu.VMEM((NK, D), bf16),
            pltpu.VMEM((NL, D), bf16),
            dma((2,)),
            pltpu.VMEM((NT // 2, 2, 2, HALF, W), f32),
            pltpu.VMEM((NK, 128), f32),
            pltpu.VMEM((NK, 128), f32),
            pltpu.VMEM((NK, 128), f32),
            pltpu.VMEM(small, f32),
            pltpu.VMEM((2, NT, 8, W), f32),
            pltpu.VMEM((2, SEATS, 2, *small), f32),
            pltpu.VMEM((SEATS, *small), f32),
            pltpu.VMEM((SEATS, *small), f32),
            pltpu.VMEM((SEATS, *small), f32),
            pltpu.VMEM((2, N_LIST, *small), f32),
            pltpu.VMEM((N_LIST, *small), f32),
            pltpu.VMEM((N_ROW, *small), f32),
            pltpu.VMEM((SEATS, *small), f32),
            pltpu.VMEM((SEATS, NK, D), bf16),
            pltpu.VMEM((SEATS, 1, NK), f32),
            pltpu.VMEM((SHARE, 128), f32),
            pltpu.VMEM((SEATS, 2, LB, W), f32),
            pltpu.VMEM((LB, NK), bf16),
            pltpu.VMEM((LB, NK), bf16),
            pltpu.VMEM((2, LB, D), f32),
            pltpu.VMEM((NCH, PIECE, D), bf16),
            pltpu.VMEM((NCH, PIECE, D), bf16),
            pltpu.VMEM((NCH, PIECE, D), bf16),
            pltpu.VMEM((2, LB, 128), f32),
            pltpu.VMEM((2, *small), f32),
            pltpu.VMEM((2, *small), f32),
            dma((2, N_LIST)), dma((2, N_LIST)), dma((N_LIST,)), dma((N_LIST,)),
            dma((N_ROW,)), dma((N_ROW,)), dma((2,)), dma((2,)),
            dma((SEATS,)), dma((SEATS,)), dma((SEATS,)), dma((SEATS,)), dma((SEATS,)), dma((SEATS,)),
            dma((20,)), dma((20,)), dma((NCH,)), dma((NCH,)), dma((NCH, 20)), dma((NCH, 20)), dma((NCH,)),
        ],
        compiler_params=pltpu.CompilerParams(
            collective_id=0, has_side_effects=True, vmem_limit_bytes=VMEM
        ),
        name="sinkhorn",
    )(key_rows, centroids)
    return new, row_pot.reshape(NK), list_pot.reshape(NL)


def solution(mesh):
    return jax.shard_map(
        local,
        mesh=mesh,
        in_specs=(P("row", None), P("list", None)),
        out_specs=(P("list", None), P("row"), P("list")),
        check_vma=False,
    )
```

```python
import math

import jax
import jax.numpy as jnp
from jax import lax
from jax.experimental import pallas as pl
from jax.experimental.pallas import tpu as pltpu
from jax.sharding import PartitionSpec as P

MESH = pl.DeviceIdType.MESH
f32 = jnp.float32
bf16 = jnp.bfloat16
LOG2E = math.log2(math.e)
LN2 = math.log(2.0)

D = 256
SCALE = 2.0 / math.sqrt(D) * LOG2E
NK = 1024
NL = 6144
W = 512
NT = NL // W
HALF = NK // 2
N_ROW, N_LIST, SEATS = 16, 8, 8
FAR_FIRST = (*range(6, 11), 5, 11, 4, 12, 13, 3, 14, 2, 15, 1)
SHARE = NL // SEATS
BLOCKS = SHARE // 128
LB = SHARE // 2
PIECE = 128
NCH = LB // PIECE
VMEM = 243 * 2**18
LOG2_KEYS = math.log2(NK * N_ROW)
LOG2_LISTS = math.log2(NL * N_LIST)
NT_DIMS = (((1,), (1,)), ((), ()))
NN_DIMS = (((1,), (0,)), ((), ()))


def tree(op, xs):
    xs = list(xs)
    while len(xs) > 1:
        ys = [op(a, b) for a, b in zip(xs[::2], xs[1::2])]
        if len(xs) % 2:
            ys.append(xs[-1])
        xs = ys
    return xs[0]


def log2(x):
    return jnp.log(x) * LOG2E


def fold(op, x):
    return tree(op, [x[8 * i : 8 * i + 8] for i in range(x.shape[0] // 8)])


def score_tile(keys, cents, scores, peak, i, half, part):
    rb = 32
    lists = pl.ds(pl.multiple_of((2 * i + half) * W, W), W)
    mine = keys[part * HALF : (part + 1) * HALF, :]
    s = lax.dot_general(mine, cents[lists, :], NT_DIMS, preferred_element_type=f32) * SCALE
    scores[i, half, part] = s
    for b in range(HALF // rb):
        rows = slice(part * HALF + b * rb, part * HALF + (b + 1) * rb)
        xs = [s[b * rb : (b + 1) * rb, v * 128 : (v + 1) * 128] for v in range(W // 128)]
        peak[rows, :] = jnp.maximum(peak[rows, :], tree(jnp.maximum, xs))


def sum_tile(scores, peak, total, i, half, part):
    rb = 32
    for b in range(HALF // rb):
        rows = slice(part * HALF + b * rb, part * HALF + (b + 1) * rb)
        top = peak[rows, :]
        xs = [scores[i, half, part, b * rb : (b + 1) * rb, v * 128 : (v + 1) * 128] for v in range(W // 128)]
        total[rows, :] += tree(jnp.add, [jnp.exp2(x - top) for x in xs])


def row_pass(work):
    def body(i, carry):
        for half in range(2):
            for step in work:
                step(i, half)
        return carry

    lax.fori_loop(0, NT // 2, body, 0)


def column_pass(scores, row_pot, stats, part, first, last):
    rb = 64
    columns = [(half, v) for half in range(2) for v in range(W // 128)]

    def body(i, carry):
        def at(n, b):
            half, v = columns[n]
            return i, half, part, slice(b * rb, (b + 1) * rb), slice(v * 128, (v + 1) * 128)

        top = None
        for n in range(len(columns) + 1):
            peaks = sums = None
            for b in range(HALF // rb):
                if n < len(columns):
                    x = scores[at(n, b)] + row_pot[part * HALF + b * rb : part * HALF + (b + 1) * rb, :]
                    scores[at(n, b)] = x
                    x = fold(jnp.maximum, x)
                    peaks = x if b == 0 else jnp.maximum(peaks, x)
                if n > 0:
                    e = jnp.exp2(scores[at(n - 1, b)] - top)
                    scores[at(n - 1, b)] = e
                    e = fold(jnp.add, e)
                    sums = e if b == 0 else sums + e
            if n > 0:
                j = i * len(columns) + n - 1
                q, row = lax.div(j, BLOCKS), lax.rem(j, BLOCKS)
                stats[part, pl.ds(q, 1), 0, pl.ds(row, 1), :] = top[None]
                stats[part, pl.ds(q, 1), 1, pl.ds(row, 1), :] = jnp.sum(sums, axis=0, keepdims=True)[None]
            if n < len(columns):
                top = jnp.max(peaks, axis=0, keepdims=True)
        return carry

    lax.fori_loop(first, last, body, 0)


def row_sums(scores, gain, total, part):
    rb, group = 64, 4

    def body(i, carry):
        def at(b):
            return pl.ds(pl.multiple_of(i * rb + 8 * b, 8), 8)

        def out(b):
            return pl.ds(pl.multiple_of(part * HALF + i * rb + 8 * b, 8), 8)

        def inner(c, accs):
            accs = list(accs)
            for t in range(group):
                for v in range(W // 128):
                    lanes = slice(v * 128, (v + 1) * 128)
                    g = gain[part, c * group + t, :, lanes]
                    for b in range(rb // 8):
                        accs[b] = accs[b] + scores[c * (group // 2) + t // 2, t % 2, part, at(b), lanes] * g
            return tuple(accs)

        zero = jnp.zeros((8, 128), f32)
        accs = lax.fori_loop(0, NT // group, inner, (zero,) * (rb // 8))
        for b in range(rb // 8):
            total[out(b), :] = accs[b]
        return carry

    lax.fori_loop(0, HALF // rb, body, 0)


def spread(compact, n, out, first=0):
    for b in range(n):
        out[first + b * 128 : first + (b + 1) * 128, :] = jnp.broadcast_to(compact[b : b + 1, :], (128, 128)).T


def remote(src, dst, send, recv, target):
    return pltpu.make_async_remote_copy(
        src_ref=src, dst_ref=dst, send_sem=send, recv_sem=recv, device_id=target, device_id_type=MESH
    )


class Gather:
    def __init__(self, at, send, recv, y, x, core, own, ring=False, lean=0):
        self.at, self.send, self.recv = at, send, recv
        self.y, self.x, self.core, self.own, self.ring = y, x, core, own, ring

        def device(dy, flip, of=core):
            return {"row": (lax.rem(y + dy + 4, 4) * 2 + (1 - x if flip else x)) * 2 + of}

        up, down, side = device(1, False), device(-1, False), device(0, True)
        self.other = device(0, False, 1 - core)
        self.moves = [
            (up, (0, False), (-1, False), None),
            (down, (0, False), (1, False), None),
            (up, (-1, False), (-2, False), 0),
            (down, (1, False), (2, False), 1),
            (side, (0, False), (0, True), None),
            (up, (0, True), (-1, True), None),
            (down, (0, True), (1, True), None),
            (side, (-2, False), (2, True), 0),
            (side, (2, False), (2, True), 1),
        ]
        if lean:
            m = 5 if lean < 0 else 6
            block = (-1, False) if lean < 0 else (1, False)
            self.moves[m] = (side, block, (block[0], True), None)
        self.lean = lean
        self.used = range(4) if ring else range(9)

    def place(self, block, part, *of):
        dy, flip = block
        return self.at(lax.rem(self.y + dy + 4, 4), 1 - self.x if flip else self.x, part, *of)

    def source(self, block, part):
        return self.own if block == (0, False) else self.place(block, part)

    def copy(self, m):
        target, sent, _, part = self.moves[m]
        return remote(self.source(sent, part), self.place(sent, part), self.send.at[m], self.recv.at[m], target)

    def arrival(self, m):
        target, _, came, part = self.moves[m]
        place = self.place(came, part)
        return remote(place, place, self.send.at[m], self.recv.at[m], target)

    def brought(self, m):
        return ((0, False), None) if m == 9 else self.moves[m][2:]

    def hand(self, m):
        block, part = self.brought(m)
        return remote(
            self.source(block, part), self.place(block, part), self.send.at[10 + m], self.recv.at[10 + m], self.other
        )

    def handed(self, m):
        block, part = self.brought(m)
        place = self.place(block, part, 1 - self.core)
        return remote(place, place, self.send.at[10 + m], self.recv.at[10 + m], self.other)

    def take(self, m, *sends):
        if m in self.used:
            self.arrival(m).wait_recv()
            for n in sends:
                if n in self.used:
                    self.copy(n).start()
            self.hand(m).start()

    def stage1(self):
        for m in (0, 1, 4):
            if m in self.used:
                self.copy(m).start()
        self.hand(9).start()

    def stage2(self):
        self.take(0, 2, *((5,) if self.lean < 0 else ()))
        self.take(1, 3, *((6,) if self.lean > 0 else ()))
        self.take(4, *((5,) if self.lean >= 0 else ()), *((6,) if self.lean <= 0 else ()))

    def stage3(self):
        self.take(2, 7)
        self.take(3, 8)

    def stage4(self):
        for m in (5, 6, 7, 8):
            self.take(m)

    def arrive(self, moves=range(10)):
        for m in moves:
            if m not in (*self.used, 9):
                continue
            self.handed(m).wait_recv()

    def sent(self):
        for m in self.used:
            self.copy(m).wait_send()
        for m in (*self.used, 9):
            self.hand(m).wait_send()


def kernel(
    keys_hbm, cents_hbm, new_ref, rowpot_ref, listpot_ref,
    keys, cents, load, scores, peak, total, row_pot, row1, gain, stats, both, pots, pots2, from_list1, from_list3, from_row2,
    row_all, keys_all, row_lanes, list_lanes, late, wa, wb, acc, give, came, done, tsum, tmine, tcame,
    list1_s, list1_r, list3_s, list3_r, row2_s, row2_r, tsum_s, tsum_r, pot_s, pot_r, pot2_s, pot2_r, all_s, all_r,
    keys_s, keys_r, twin_s, twin_r, out_s, out_r, here,
):
    row, lst = lax.axis_index("row"), lax.axis_index("list")
    core, x, y = lax.rem(row, 2), lax.rem(lax.div(row, 2), 2), lax.div(row, 4)
    seat = y * 2 + core

    def device(at, x):
        return (lax.div(at, 2) * 2 + x) * 2 + lax.rem(at, 2)

    def seat_of(device):
        return lax.div(device, 4) * 2 + lax.rem(device, 2)

    barrier = pltpu.get_barrier_semaphore()
    for k in range(1, N_ROW):
        pl.semaphore_signal(barrier, inc=1, device_id={"row": lax.rem(row + k, N_ROW)}, device_id_type=MESH)
    for k in range(1, N_LIST):
        pl.semaphore_signal(barrier, inc=1, device_id={"list": lax.rem(lst + k, N_LIST)}, device_id_type=MESH)
    stats[...] = jnp.ones(stats.shape, f32)
    tmine[...] = jnp.zeros(tmine.shape, f32)
    pots2[...] = jnp.zeros(pots2.shape, f32)
    peak[...] = jnp.full(peak.shape, -1e30, f32)
    total[...] = jnp.zeros(total.shape, f32)
    loads = [
        pltpu.make_async_copy(keys_hbm, keys, load.at[0]),
        pltpu.make_async_copy(cents_hbm, cents, load.at[1]),
    ]
    for copy in loads:
        copy.start()

    def score(part):
        return lambda i, half: score_tile(keys, cents, scores, peak, i, half, part)

    def add(part):
        return lambda i, half: sum_tile(scores, peak, total, i, half, part)

    n = HALF // 128

    def prepare(part):
        for b in range(n):
            rows = slice(part * HALF + b * 128, part * HALF + (b + 1) * 128)
            top = peak[rows, :].T
            best = jnp.max(top, axis=0, keepdims=True)
            from_list1[part, lst, b : b + 1, :] = best
            from_list1[part, lst, n + b : n + b + 1, :] = jnp.sum(
                total[rows, :].T * jnp.exp2(top - best), axis=0, keepdims=True
            )

    for copy in loads:
        copy.wait()
    keys_all[seat] = keys[...]
    row_pass([score(0)])
    row_pass([score(1), add(0)])
    prepare(0)
    pl.semaphore_wait(barrier, N_ROW + N_LIST - 2)

    def keys_at(y, x, part, of=core):
        at = y * 2 + of
        return keys_all.at[at] if part is None else keys_all.at[at, pl.ds(part * (NK // 2), NK // 2)]

    gather = Gather(keys_at, keys_s, keys_r, y, x, core, keys, ring=True)
    gather.stage1()
    sent = []

    def start(copies):
        for copy in copies:
            copy.start()
            sent.append(copy)

    def to_list(buf, send, recv):
        start(
            remote(buf.at[lst], buf.at[lst], send.at[k], recv.at[lst], {"list": lax.rem(lst + k, N_LIST)})
            for k in (5, 3, 7, 1, 4, 6, 2)
        )

    def from_list(buf, send, recv):
        for k in range(1, N_LIST):
            src = lax.rem(lst + k, N_LIST)
            remote(buf.at[src], buf.at[src], send.at[k], recv.at[src], {"list": src}).wait_recv()

    def to_row(src_of, buf, send, recv):
        to = [lax.rem(row + k, N_ROW) for k in FAR_FIRST]
        start(
            remote(src_of.at[seat_of(t)], buf.at[row], send.at[k + 1], recv.at[row], {"row": t})
            for k, t in enumerate(to)
        )

    def from_row(buf, send, recv):
        for k in range(1, N_ROW):
            src = lax.rem(row + k, N_ROW)
            remote(buf.at[src], buf.at[src], send.at[k], recv.at[src], {"row": src}).wait_recv()

    def to_seats(buf, send, recv):
        to = [lax.rem(seat + k, SEATS) for k in (4, 5, 3, 6, 2, 7, 1)]
        start(
            remote(buf.at[seat], buf.at[seat], send.at[k + 1], recv.at[seat], {"row": device(t, x)})
            for k, t in enumerate(to)
        )

    def from_seats(buf, send, recv):
        for k in range(1, SEATS):
            src = lax.rem(seat + k, SEATS)
            remote(buf.at[src], buf.at[src], send.at[k], recv.at[src], {"row": device(src, x)}).wait_recv()

    def tell(part):
        to_list(from_list1.at[part], list1_s.at[part], list1_r.at[part])

    def learn(part):
        from_list(from_list1.at[part], list1_s.at[part], list1_r.at[part])
        best = tree(jnp.maximum, [from_list1[part, k, 0:n] for k in range(N_LIST)])
        whole = tree(
            jnp.add, [from_list1[part, k, n : 2 * n] * jnp.exp2(from_list1[part, k, 0:n] - best) for k in range(N_LIST)]
        )
        row1[part * n : (part + 1) * n, :] = -LOG2_KEYS - (best + log2(whole))
        spread(row1[part * n : (part + 1) * n, :], n, row_pot, part * HALF)

    tell(0)
    row_pass([add(1)])
    prepare(1)
    tell(1)

    learn(0)
    column_pass(scores, row_pot, stats, 0, 0, NT // 2)
    learn(1)
    column_pass(scores, row_pot, stats, 1, 0, NT // 2)
    for q in range(SEATS):
        best = jnp.maximum(stats[0, q, 0], stats[1, q, 0])
        both[q] = best + log2(tree(jnp.add, [stats[p, q, 1] * jnp.exp2(stats[p, q, 0] - best) for p in range(2)]))
    from_row2[row] = both[seat]
    to_row(both, from_row2, row2_s, row2_r)
    from_row(from_row2, row2_s, row2_r)
    best = tree(jnp.maximum, [from_row2[k] for k in range(N_ROW)])
    whole = tree(jnp.add, [jnp.exp2(from_row2[k] - best) for k in range(N_ROW)])
    pots[seat] = -LOG2_LISTS - (best + log2(whole))
    to_seats(pots, pot_s, pot_r)
    from_seats(pots, pot_s, pot_r)
    gather.stage2()

    for q in range(SEATS):
        for p in range(2):
            g = jnp.exp2(stats[p, q, 0] + pots[q])
            for b in range(BLOCKS):
                j = q * BLOCKS + b
                v = j % (W // 128)
                gain[p, j // (W // 128), :, v * 128 : (v + 1) * 128] = jnp.broadcast_to(g[b : b + 1, :], (8, 128))
    row_sums(scores, gain, total, 0)
    row_sums(scores, gain, total, 1)
    for b in range(NK // 128):
        from_list3[lst, b : b + 1, :] = jnp.sum(total[b * 128 : (b + 1) * 128, :].T, axis=0, keepdims=True)
    to_list(from_list3, list3_s, list3_r)

    firsts = ((1 - x) * LB, x * LB)

    def seat_at(k):
        j = lax.div(k, 2)
        far = j + lax.div(j, 2) - 2 * lax.div(j, 3)
        return lax.rem(y + far, 4) * 2 + lax.rem(k, 2)

    spread(pots[seat] + LOG2_LISTS, BLOCKS, list_lanes)

    def late_scores(k, carry):
        tile = keys_all[seat_at(k)]
        for side_ in range(2):
            lists = pl.ds(pl.multiple_of(seat * SHARE + firsts[side_], 128), LB)
            for h in range(2):
                s = lax.dot_general(cents[lists, :], tile[h * W : (h + 1) * W], NT_DIMS, preferred_element_type=f32)
                c = list_lanes[pl.ds(pl.multiple_of(firsts[side_], 128), LB), :]
                for v in range(W // 128):
                    lanes = slice(v * 128, (v + 1) * 128)
                    if side_ == 0:
                        late[k, h, :, lanes] = s[:, lanes] * SCALE + c
                    else:
                        scores[lax.div(k, 2), lax.rem(k, 2), h, 0:LB, lanes] = s[:, lanes] * SCALE + c
        return carry

    gather.arrive((0, 1, 9))
    lax.fori_loop(0, 4, late_scores, 0)
    from_list(from_list3, list3_s, list3_r)
    delta = -LOG2_KEYS - log2(tree(jnp.add, [from_list3[k] for k in range(N_LIST)]))
    row2 = row1[...] + delta
    row_all[seat] = row2
    to_seats(row_all, all_s, all_r)
    rowpot_ref[...] = row2 * LN2
    acc[...] = jnp.zeros(acc.shape, f32)
    tsum[...] = jnp.zeros(tsum.shape, f32)
    gather.stage3()
    gather.arrive((2, 3))
    lax.fori_loop(4, SEATS, late_scores, 0)

    def piece_at(ch):
        def at(y, x, part, of=core):
            first = pl.multiple_of((y * 2 + of) * SHARE + x * LB + ch * PIECE, PIECE)
            if part is None:
                return new_ref.at[pl.ds(first, PIECE)]
            return new_ref.at[pl.ds(pl.multiple_of(first + part * (PIECE // 2), PIECE // 2), PIECE // 2)]

        return at

    outs = [
        Gather(piece_at(ch), out_s.at[ch], out_r.at[ch], y, x, core, done.at[ch], lean=(1, -1, 0)[ch])
        for ch in range(NCH)
    ]
    side = {"row": device(seat, 1 - x)}

    def swap(ch):
        return remote(give.at[ch], came.at[ch], twin_s.at[ch], twin_r.at[ch], side)

    def swap_sums(block):
        return remote(tmine.at[block], tcame.at[block], tsum_s.at[block], tsum_r.at[block], side)

    def sums(side_, pieces):
        for b in pieces:
            rows = slice(b * 128, (b + 1) * 128)
            tmine[side_, b : b + 1, :] = jnp.sum(tsum[side_, rows, :].T, axis=0, keepdims=True)

    def hand_over():
        sums(0, range(NCH))
        swap_sums(0).start()
        for ch in range(NCH):
            give[ch] = acc[0, ch * PIECE : (ch + 1) * PIECE, :].astype(bf16)
            swap(ch).start()

    def keep(ch):
        return pltpu.make_async_copy(done.at[ch], piece_at(ch)(y, x, None), here.at[ch])

    def begin(ch):
        whole = tmine[1, ch : ch + 1, :] + tcame[0, ch : ch + 1, :]
        scale = jnp.broadcast_to(1.0 / whole, (PIECE, 128)).T
        swap(ch).wait()
        for v in range(D // 128):
            lanes = slice(v * 128, (v + 1) * 128)
            summed = acc[1, ch * PIECE : (ch + 1) * PIECE, lanes] + came[ch, :, lanes].astype(f32)
            done[ch, :, lanes] = (summed * scale).astype(bf16)
        outs[ch].stage1()
        keep(ch).start()

    def update(block, other):
        for b in range(NCH):
            at = pl.ds((x if block else 1 - x) * NCH + b, 1)
            whole = tmine[block, b : b + 1, :] + tcame[other, b : b + 1, :]
            pots2[seat, at, :] = pots[seat, at, :] - log2(whole)

    def run(side_):
        def sum_up(w_ref, k):
            return lax.dot_general(w_ref[...], keys_all[seat_at(k)], NN_DIMS, preferred_element_type=f32)

        def weigh(w_ref, k, odd):
            parts = []
            for v in range(NK // 128):
                h, u = v // (W // 128), v % (W // 128)
                lanes = slice(u * 128, (u + 1) * 128)
                s = late[k, h, :, lanes] if side_ == 0 else scores[lax.div(k, 2), odd, h, 0:LB, lanes]
                r = row_lanes[k, :, v * 128 : (v + 1) * 128]
                w = jnp.exp2(s + r)
                w_ref[:, v * 128 : (v + 1) * 128] = w.astype(bf16)
                parts.append(w)
            tsum[side_] += tree(jnp.add, parts)

        def step(i, carry):
            before = sum_up(wb, lax.rem(2 * i + SEATS - 1, SEATS))
            weigh(wa, 2 * i, 0)
            acc[side_] += before
            now = sum_up(wa, 2 * i)
            weigh(wb, 2 * i + 1, 1)
            acc[side_] += now
            return carry

        wb[...] = jnp.zeros(wb.shape, bf16)
        lax.fori_loop(0, SEATS // 2, step, 0)
        acc[side_] += sum_up(wb, SEATS - 1)

    from_seats(row_all, all_s, all_r)
    for k in range(SEATS):
        for b in range(NK // 128):
            row_lanes[k, :, b * 128 : (b + 1) * 128] = row_all[seat_at(k), b : b + 1, :]
    run(0)
    hand_over()
    run(1)
    sums(1, range(NCH))
    swap_sums(0).wait()
    for ch in range(NCH):
        begin(ch)
    swap_sums(1).start()
    for ch in range(NCH):
        outs[ch].stage2()
    outs[0].stage3()
    swap_sums(1).wait()
    update(0, 1)
    update(1, 0)
    to_seats(pots2, pot2_s, pot2_r)
    outs[1].stage3()
    outs[0].stage4()
    outs[2].stage3()
    outs[1].stage4()
    outs[2].stage4()
    from_seats(pots2, pot2_s, pot2_r)
    for q in range(SEATS):
        listpot_ref[q * BLOCKS : (q + 1) * BLOCKS, :] = pots2[q, 0:BLOCKS, :] * LN2
    for ch in range(NCH):
        keep(ch).wait()
        outs[ch].arrive()
        outs[ch].sent()
    gather.sent()
    for copy in sent:
        copy.wait_send()


def local(key_rows, centroids):
    vmem = pl.BlockSpec(memory_space=pltpu.VMEM)
    dma = pltpu.SemaphoreType.DMA
    small = (8, 128)
    new, row_pot, list_pot = pl.pallas_call(
        kernel,
        out_shape=(
            pltpu.VMEM((NL, D), bf16),
            jax.ShapeDtypeStruct(small, f32),
            jax.ShapeDtypeStruct((NL // 128, 128), f32),
        ),
        in_specs=[pl.BlockSpec(memory_space=pltpu.HBM)] * 2,
        out_specs=(pl.BlockSpec(memory_space=pl.ANY), vmem, vmem),
        scratch_shapes=[
            pltpu.VMEM((NK, D), bf16),
            pltpu.VMEM((NL, D), bf16),
            dma((2,)),
            pltpu.VMEM((NT // 2, 2, 2, HALF, W), f32),
            pltpu.VMEM((NK, 128), f32),
            pltpu.VMEM((NK, 128), f32),
            pltpu.VMEM((NK, 128), f32),
            pltpu.VMEM(small, f32),
            pltpu.VMEM((2, NT, 8, W), f32),
            pltpu.VMEM((2, SEATS, 2, *small), f32),
            pltpu.VMEM((SEATS, *small), f32),
            pltpu.VMEM((SEATS, *small), f32),
            pltpu.VMEM((SEATS, *small), f32),
            pltpu.VMEM((2, N_LIST, *small), f32),
            pltpu.VMEM((N_LIST, *small), f32),
            pltpu.VMEM((N_ROW, *small), f32),
            pltpu.VMEM((SEATS, *small), f32),
            pltpu.VMEM((SEATS, NK, D), bf16),
            pltpu.VMEM((SEATS, 1, NK), f32),
            pltpu.VMEM((SHARE, 128), f32),
            pltpu.VMEM((SEATS, 2, LB, W), f32),
            pltpu.VMEM((LB, NK), bf16),
            pltpu.VMEM((LB, NK), bf16),
            pltpu.VMEM((2, LB, D), f32),
            pltpu.VMEM((NCH, PIECE, D), bf16),
            pltpu.VMEM((NCH, PIECE, D), bf16),
            pltpu.VMEM((NCH, PIECE, D), bf16),
            pltpu.VMEM((2, LB, 128), f32),
            pltpu.VMEM((2, *small), f32),
            pltpu.VMEM((2, *small), f32),
            dma((2, N_LIST)), dma((2, N_LIST)), dma((N_LIST,)), dma((N_LIST,)),
            dma((N_ROW,)), dma((N_ROW,)), dma((2,)), dma((2,)),
            dma((SEATS,)), dma((SEATS,)), dma((SEATS,)), dma((SEATS,)), dma((SEATS,)), dma((SEATS,)),
            dma((20,)), dma((20,)), dma((NCH,)), dma((NCH,)), dma((NCH, 20)), dma((NCH, 20)), dma((NCH,)),
        ],
        compiler_params=pltpu.CompilerParams(
            collective_id=0, has_side_effects=True, vmem_limit_bytes=VMEM
        ),
        name="sinkhorn",
    )(key_rows, centroids)
    return new, row_pot.reshape(NK), list_pot.reshape(NL)


def solution(mesh):
    return jax.shard_map(
        local,
        mesh=mesh,
        in_specs=(P("row", None), P("list", None)),
        out_specs=(P("list", None), P("row"), P("list")),
        check_vma=False,
    )
```
